256 devices in a mesh: row: 64 (over z, x, core), col: 4 (over y).
Axes of the slice: x: 4, y: 4, z: 8, core: 2. Of those that a mesh axis runs over, the one named last changes fastest.
Arguments:
- y_prev: float32 [32768, 128], P(('row', 'col'))
- step_prev: float32 [32768, 128], P(('row', 'col')), may hold values from -3 to 3
- accept: int32 [256], P(('row', 'col')), may hold values 0 or 1
- blocks: bfloat16 [64, 4, 192, 128, 128], P('row', 'col'), as said below
- blk_row: int32 [64, 4, 192], P('row', 'col'), may hold values from 0 to 3
- blk_col: int32 [64, 4, 192], P('row', 'col'), may hold values from 0 to 63
Outputs:
- step: float32 [32768, 128], P(('row', 'col'))
- residual: float32 [32768, 128], P(('row', 'col'))
The draws below stay inside these ranges and needn't reach their ends.
Inputs may be any that keep to these rules, and one draw needn't show every extreme that they name: `blocks`: edge weights.
All inputs are finite; a program needn't handle non-finite values. No bound on the sum of `accept` on one device may be relied on, other than what follows from the above.
Results may differ from the reference program's by a relative error of at most 0.035.
Values may be sent and summed in bfloat16 or wider, within the bound.
A program may use at most 64 MiB of HBM per device.

```python
import math
import jax
import jax.numpy as jnp
import numpy as np
from jax import lax

R = 128
BLK = 128
ROWB = 4
SLOTS = 192
ITERS = 3
BPD = 1
N = 32768
N_ROW = 64
N_COL = 4


def draw_y_prev(key, part):
    key = jax.random.fold_in(key, 7)
    key_common, key_noise = jax.random.split(key)
    common = jnp.clip(2.0 * jax.random.normal(key_common, (R,), jnp.float32), -6.0, 6.0)
    noise = jnp.clip(jax.random.normal(key_noise, (N, R), jnp.float32), -6.0, 6.0)
    return common[None, :] + noise


def draw_blocks(key, part):
    key = jax.random.fold_in(key, 5)
    key_noise, key_level = jax.random.split(key)
    fan = SLOTS * N_COL * BLK / ROWB
    root = math.sqrt(fan)
    jitter = jax.random.uniform(key_level, (N_ROW,), jnp.float32)
    position = (jnp.arange(N_ROW, dtype=jnp.float32) + jitter) / N_ROW
    shape = (N_ROW, N_COL, SLOTS, BLK, BLK)
    level = -6.0 + 8.0 * position
    noise = jnp.clip(jax.random.normal(key_noise, shape, jnp.float32), -6.0, 6.0)
    values = (noise + level[:, None, None, None, None] / root) / root
    return values.astype(jnp.bfloat16)


def touch_ends(values, key, low, largest):
    shape = values.shape
    spot = [jax.random.randint(jax.random.fold_in(key, axis), (), 0, shape[axis]) for axis in range(len(shape))]
    values = values.at[tuple(spot)].set(low)
    longest = shape.index(max(shape))
    spot[longest] = (spot[longest] + 1) % shape[longest]
    return values.at[tuple(spot)].set(largest)


def levels(stream_key, dims, cuts, least, top_value):
    level = 1.0
    for axis_at, blocks in cuts:
        heights = jax.random.uniform(jax.random.fold_in(jax.random.fold_in(stream_key, 6), axis_at), (blocks,), jnp.float32, least / len(cuts), top_value / len(cuts))
        level = level * jnp.repeat(jnp.exp(heights), dims[axis_at] // blocks).reshape((-1,) + (1,) * (len(dims) - 1 - axis_at))
    return level


def cumulative_ranks(number_of, lean):
    weights = [(1 << 20) // math.isqrt(rank ** lean) + 1 for rank in range(1, number_of + 1)]
    scale = 1 + sum(weights) // (1 << 30)
    return np.cumsum(np.array([max(1, weight // scale) for weight in weights]))


def ranked(key, dims, count, slope):
    table = cumulative_ranks(count, slope)
    pick = jax.random.randint(jax.random.fold_in(key, 1), dims, 0, int(table[count - 1]))
    rank = jnp.searchsorted(jnp.asarray(table, jnp.int32), pick, side="right")
    return jax.random.permutation(jax.random.fold_in(key, 2), count)[rank].astype(jnp.int32)


def gaussian(key, dims, spread, bound, cuts=(), kind=jnp.bfloat16):
    values = jax.random.normal(key, dims, jnp.float32) * spread
    if len(cuts) > 0:
        values = levels(key, dims, cuts, -0.22, 0.18) * values
    return jnp.clip(values, min=-bound, max=bound).astype(kind)


def setup_inputs(seed: int = 0) -> dict:
    key_list = jax.random.split(jax.random.key(seed), 7)
    return {
        "y_prev": draw_y_prev(jax.random.fold_in(key_list[6], 71), 0),
        "step_prev": gaussian(key_list[1], (N, R), 0.5, 3.0, ((0, 256),), jnp.float32),
        "accept": touch_ends((jax.random.randint(key_list[2], (N // BLK,), 0, 2) < 1).astype(jnp.int32), jax.random.fold_in(key_list[2], 1), 0, 1),
        "blocks": draw_blocks(jax.random.fold_in(key_list[6], 71), 0),
        "blk_row": touch_ends(jax.random.randint(key_list[4], (N_ROW, N_COL, SLOTS), 0, ROWB), jax.random.fold_in(key_list[4], 1), 0, ROWB - 1).astype(jnp.int32),
        "blk_col": touch_ends(ranked(key_list[5], (N_ROW, N_COL, SLOTS), N_ROW * BPD, 1), jax.random.fold_in(key_list[5], 3), 0, (N_ROW * BPD) - 1).astype(jnp.int32),
    }


damping = 14.0

def normalize(rows):
    return rows * lax.rsqrt(lax.optimization_barrier(jnp.sum(rows * rows, axis=1, keepdims=True)) + 1e-06)

def product(field_bf, blocks, blk_row, blk_col):
    tiles = field_bf.reshape(-1, BLK, R)

    def one_group(group):
        total = jnp.zeros((ROWB, BLK, R), jnp.float32)
        for column in range(N_COL):
            local = blk_col[group, column]
            where = (local // BPD * N_COL + column) * BPD + local % BPD
            picked = tiles[where.astype(jnp.int32)].astype(jnp.float32)
            prods = jnp.einsum('sab,sbd->sad', blocks[group, column].astype(jnp.float32), picked)
            onehot = (blk_row[group, column][None, :] == jnp.arange(ROWB, dtype=jnp.int32)[:, None]).astype(jnp.float32)
            total = total + jnp.einsum('rs,sad->rad', onehot, prods)
        return total
    out = lax.map(one_group, jnp.arange(N_ROW, dtype=jnp.int32))
    return out.reshape(N, R)

def reference(y_prev, step_prev, accept, blocks, blk_row, blk_col):
    taken = accept.astype(jnp.float32)[:, None, None]
    moved = y_prev.reshape(-1, BLK, R) + taken * step_prev.reshape(-1, BLK, R)
    point = normalize(moved.reshape(N, R))
    full_grad = 2.0 * product(point.astype(jnp.bfloat16), blocks, blk_row, blk_col)
    lam = lax.optimization_barrier(jnp.sum(point * full_grad, axis=1, keepdims=True))
    grad = full_grad - lam * point

    def hessian(vector):
        image = 2.0 * product(vector.astype(jnp.bfloat16), blocks, blk_row, blk_col)
        image = image - lax.optimization_barrier(jnp.sum(point * image, axis=1, keepdims=True)) * point
        return image - lam * vector + damping * vector
    residual = -grad
    direction = residual
    step = jnp.zeros_like(residual)
    norm_now = jnp.sum(residual * residual)
    for turn in range(ITERS):
        image = hessian(direction)
        alpha = norm_now / jnp.sum(direction * image)
        step = step + alpha * direction
        residual = residual - alpha * image
        norm_next = jnp.sum(residual * residual)
        direction = residual + norm_next / norm_now * direction
        norm_now = norm_next
    return (step, residual)
```

```python
import functools

import jax
import jax.numpy as jnp
from jax import lax
from jax.experimental import pallas as pl
from jax.experimental.pallas import tpu as pltpu
from jax.sharding import PartitionSpec as P

MESH = pl.DeviceIdType.MESH
ITERS = 3
DAMPING = 14.0
NZ, NX, NY = 8, 4, 4
SIDE = 128
GROUP = 4
TILES = 64
Z_ORDER = (1, 7, 2, 6, 3, 5, 4)
X_ORDER = (2, 1, 3)
D_ORDER = (0,) + Z_ORDER
PAIRS = ((0, 0), (0, 1), (0, 2), (1, 1), (1, 2), (2, 2), (0, 3), (1, 3), (2, 3))
F32 = jnp.float32
BF16 = jnp.bfloat16
I32 = jnp.int32


def device(z, x, core, y):
    return ((z % NZ * NX + x % NX) * 2 + core % 2, y % NY)


def row_sum(a):
    return jnp.sum(a, axis=1, keepdims=True)


def slot_plan(rows, cols, z, x, core):
    slots = rows.shape[1]
    far = jnp.concatenate([rows, jnp.zeros((1, 256 - slots), I32)], axis=1)
    col = jnp.concatenate([cols, jnp.zeros((1, 256 - slots), I32)], axis=1)
    lane = lax.broadcasted_iota(I32, (1, 256), 1)
    dz = (z + NZ - col // 8) % NZ
    dx = (x + NX - (col // 2) % NX) % NX
    rel = (col + core) % 2
    key_row = jnp.where(lane < slots, ((rel * NZ + dz) * NX + dx) * GROUP + far, 1 << 12)
    sub2 = lax.broadcasted_iota(I32, (256, 256), 0)
    lane2 = lax.broadcasted_iota(I32, (256, 256), 1)
    key_r = jnp.broadcast_to(key_row, (256, 256))
    key_col = jnp.sum(jnp.where(sub2 == lane2, key_r, 0), axis=1, keepdims=True)
    key_c = jnp.broadcast_to(key_col, (256, 256))
    same_before = jnp.sum(jnp.where((key_r == key_c) & (lane2 < sub2), 1, 0), axis=1, keepdims=True)
    place = same_before + jnp.sum(jnp.where(key_r < key_c, 1, 0), axis=1, keepdims=True)
    here = jnp.broadcast_to(place, (256, 256)) == lane2
    order = jnp.sum(jnp.where(here, sub2, 0), axis=0, keepdims=True)
    keep = jnp.sum(jnp.where(here & (jnp.broadcast_to(same_before, (256, 256)) > 0), 1, 0), axis=0, keepdims=True)
    upto = jnp.sum(jnp.where(key_c <= lane2, 1, 0), axis=0, keepdims=True)
    found = jnp.sum(jnp.where(key_c == lane2, 1, 0), axis=0, keepdims=True)
    last = jnp.where(found > 0, upto - 1, slots)
    return jnp.concatenate([order, keep, last, jnp.zeros((5, 256), I32)], axis=0)


def kernel(
    slots, y_ref, step_ref, accept_ref, row_ref, col_ref, blocks_ref, out_step, out_res,
    raw, comp, dense, gat, acc, point, lam, vs, part, got, ar_own, ar_buf, theta, plan_v, plan_s,
    local_sem, gs, zr, xr, cr, ps, pr, ars, arr,
):
    row = lax.axis_index("row")
    y = lax.axis_index("col")
    z, x, core = row // (2 * NX), row // 2 % NX, row % 2

    first = [(dz, dk) for dz in range(NZ) for dk in range(2)]
    second = [(dx, dy) for dx in range(NX) for dy in range(NY)]
    peers = [[device(z + dz, x, core + dk, y) for dz, dk in first], [device(z, x + dx, core, y + dy) for dx, dy in second]]

    barrier = pltpu.get_barrier_semaphore()
    for stage in range(2):
        for peer in peers[stage][1:]:
            pl.semaphore_signal(barrier, inc=1, device_id=peer, device_id_type=MESH)
    blocks_copy = pltpu.make_async_copy(blocks_ref, raw, local_sem.at[0])
    blocks_copy.start()

    moved = y_ref[...] + accept_ref[0].astype(F32) * step_ref[...]
    unit = moved * lax.rsqrt(row_sum(moved * moved) + 1e-06)
    point[...] = unit
    gat[0, 0] = unit.astype(BF16)
    vs[0] = jnp.zeros((SIDE, SIDE), F32)
    lam[...] = jnp.zeros((SIDE, SIDE), F32)
    theta[...] = jnp.zeros((8, SIDE), F32)
    plan_v[...] = slot_plan(row_ref[...], col_ref[...], z, x, core)
    plan_copy = pltpu.make_async_copy(plan_v, plan_s, local_sem.at[1])
    plan_copy.start()
    comp[slots] = jnp.zeros((SIDE, SIDE), BF16)
    pl.semaphore_wait(barrier, len(first) + len(second) - 2)

    def remote(src, dst, send, recv, peer):
        return pltpu.make_async_remote_copy(
            src_ref=src, dst_ref=dst, send_sem=send, recv_sem=recv, device_id=peer, device_id_type=MESH
        )

    def reduce_send(use, stage):
        for j in range(1, 16):
            remote(
                ar_own.at[use, stage], ar_buf.at[use, stage, j], ars.at[use, stage], arr.at[use, stage], peers[stage][j]
            ).start()

    def reduce_take(use, stage):
        for sem in (arr, ars):
            whole = ar_buf.at[use, stage, pl.ds(1, 15)]
            pltpu.make_async_copy(whole, whole, sem.at[use, stage]).wait()
        return ar_own[use, stage] + jnp.sum(ar_buf[use, stage, 1:16], axis=0)

    def compact(start, count):
        def one(j, total):
            keep = plan_s[1, j].astype(F32)
            total = keep * total + raw[plan_s[0, j]].astype(F32)
            comp[j] = total.astype(BF16)
            return total

        return functools.partial(lax.fori_loop, start, start + count, one)

    def densify(chunk):
        def one(q, carry):
            dx, r = q // GROUP, q % GROUP
            dense[chunk, pl.ds(r * SIDE, SIDE), :] = jnp.concatenate(
                [comp[plan_s[2, chunk * 16 + i * GROUP + r]] for i in range(NX)], axis=1
            )
            return carry

        def rows(r, carry):
            return one(r, carry)

        lax.fori_loop(0, GROUP, rows, 0)

    def product(k, carry):
        p = k % 2

        def tile(d, dx):
            return gat.at[p, d * NX + dx]

        def z_copy(d):
            return remote(tile(0, 0), tile(d, 0), gs.at[p], zr.at[p, d], device(z + d, x, core, y))

        def x_copy(d, dx):
            return remote(tile(d, 0), tile(d, dx), gs.at[p], xr.at[p, d, dx], device(z, x + dx, core, y))

        def relay(d):
            return remote(
                gat.at[p, pl.ds(d * NX, NX)], gat.at[p, pl.ds(32 + d * NX, NX)], gs.at[p], cr.at[p, d],
                device(z, x, core + 1, y),
            )

        for d in Z_ORDER:
            z_copy(d).start()
        for dx in X_ORDER:
            x_copy(0, dx).start()

        @pl.when(k == 1)
        def _():
            reduce_send(0, 0)

        @pl.when(k == 0)
        def _():
            plan_copy.wait()
            blocks_copy.wait()

        acc[...] = jnp.zeros((GROUP * SIDE, SIDE), F32)
        chunk = slots // 8
        for i, d in enumerate(Z_ORDER):

            @pl.when(k == 0)
            def _():
                compact_from(i * chunk, chunk)

            z_copy(d).wait_recv()
            for dx in X_ORDER:
                x_copy(d, dx).start()

        @pl.when(k == 0)
        def _():
            compact_from(7 * chunk, slots - 7 * chunk)

        @pl.when(k == 1)
        def _():
            ar_own[0, 1] = reduce_take(0, 0)
            reduce_send(0, 1)

        for d in D_ORDER:
            for dx in X_ORDER:
                x_copy(d, dx).wait_recv()
            relay(d).start()

            @pl.when(k == 0)
            def _():
                densify(d)

            acc[...] += jnp.dot(
                dense[d], gat[p, d * NX : d * NX + NX].reshape(NX * SIDE, SIDE), preferred_element_type=F32
            )
        for d in D_ORDER:

            @pl.when(k == 0)
            def _():
                densify(NZ + d)

            relay(d).wait_recv()
            acc[...] += jnp.dot(
                dense[NZ + d], gat[p, 32 + d * NX : 32 + d * NX + NX].reshape(NX * SIDE, SIDE),
                preferred_element_type=F32,
            )

        part[p] = acc[...].astype(BF16).reshape(GROUP, SIDE, SIDE)

        def part_copy(dy):
            return remote(part.at[p, (y + dy) % NY], got.at[p, dy], ps.at[p], pr.at[p, dy], device(z, x, core, y + dy))

        for dy in (2, 1, 3):
            part_copy(dy).start()
        sent = gat.at[p, pl.ds(0, 63)]
        pltpu.make_async_copy(sent, sent, gs.at[p]).wait()

        @pl.when(k == 1)
        def _():
            sums = reduce_take(0, 1)
            theta[...] = jnp.broadcast_to(DAMPING - sums[0:1] / sums[1:2], (8, SIDE))

        own = acc[pl.ds(pl.multiple_of(y * SIDE, SIDE), SIDE), :]
        for dy in (1, 3, 2):
            part_copy(dy).wait_recv()
            own = own + got[p, dy].astype(F32)
        full = 2.0 * own
        unit = point[...]
        lean = row_sum(unit * full)
        flat = full - lean * unit
        lam[...] = jnp.where(k == 0, jnp.broadcast_to(lean, (SIDE, SIDE)), lam[...])
        before = vs[jnp.maximum(k - 1, 0)]
        new = jnp.where(k == 0, -flat, flat + (DAMPING - theta[0:1, :] - lam[...]) * before)
        vs[k] = new
        gat[1 - p, 0] = new.astype(BF16)

        @pl.when(k == 0)
        def _():
            square = new * new
            rows = jnp.concatenate(
                [jnp.sum(lam[...] * square, axis=0, keepdims=True), jnp.sum(square, axis=0, keepdims=True),
                 jnp.zeros((14, SIDE), F32)], axis=0)
            ar_own[0, 0] = jnp.broadcast_to(row_sum(rows), (16, SIDE))

        sent2 = part.at[p, pl.ds(0, 3)]
        pltpu.make_async_copy(sent2, sent2, ps.at[p]).wait()
        return carry

    def compact_from(start, count):
        total = compact(start, count)(total_get())
        out_res[...] = total

    def total_get():
        return out_res[...]

    out_res[...] = jnp.zeros((SIDE, SIDE), F32)
    lax.fori_loop(0, ITERS + 1, product, 0)

    grams = [jnp.sum(vs[i] * vs[j], axis=0, keepdims=True) for i, j in PAIRS]
    rows = jnp.concatenate(grams + [jnp.zeros((16 - len(PAIRS), SIDE), F32)], axis=0)
    ar_own[1, 0] = jnp.broadcast_to(row_sum(rows), (16, SIDE))
    reduce_send(1, 0)
    ar_own[1, 1] = reduce_take(1, 0)
    reduce_send(1, 1)
    total = reduce_take(1, 1)
    gram = {pair: total[e : e + 1, :] for e, pair in enumerate(PAIRS)}
    shift = theta[0:1, :]

    def dot(a, b):
        terms = [a[i] * b[j] * gram[(min(i, j), max(i, j))] for i in a for j in b]
        return functools.reduce(lambda s, t: s + t, terms)

    def axpy(a, scale, b):
        out = dict(a)
        for i, v in b.items():
            out[i] = out[i] + scale * v if i in out else scale * v
        return out

    one = jnp.ones((1, SIDE), F32)
    residual = {0: one}
    direction = {0: one}
    step = {}
    norm_now = dot(residual, residual)
    for turn in range(ITERS):
        image = {i + 1: v for i, v in direction.items()}
        image = axpy(image, shift, direction)
        alpha = norm_now / dot(direction, image)
        step = axpy(step, alpha, direction)
        residual = axpy(residual, -alpha, image)
        if turn < ITERS - 1:
            norm_next = dot(residual, residual)
            direction = axpy(residual, norm_next / norm_now, direction)
            norm_now = norm_next
    out_step[...] = functools.reduce(lambda s, t: s + t, [step[i] * vs[i] for i in sorted(step)])
    out_res[...] = functools.reduce(lambda s, t: s + t, [residual[i] * vs[i] for i in sorted(residual)])


def shards(y_prev, step_prev, accept, blocks, blk_row, blk_col):
    tiles = blocks[0, 0]
    slots = tiles.shape[0]
    vmem = pl.BlockSpec(memory_space=pltpu.VMEM)
    return pl.pallas_call(
        functools.partial(kernel, slots),
        out_shape=[jax.ShapeDtypeStruct(y_prev.shape, F32)] * 2,
        in_specs=[vmem, vmem, pl.BlockSpec(memory_space=pltpu.SMEM), vmem, vmem, pl.BlockSpec(memory_space=pl.ANY)],
        out_specs=[vmem, vmem],
        scratch_shapes=[
            pltpu.VMEM((slots, SIDE, SIDE), BF16),
            pltpu.VMEM((slots + 1, SIDE, SIDE), BF16),
            pltpu.VMEM((16, GROUP * SIDE, NX * SIDE), BF16),
            pltpu.VMEM((2, TILES, SIDE, SIDE), BF16),
            pltpu.VMEM((GROUP * SIDE, SIDE), F32),
            pltpu.VMEM((SIDE, SIDE), F32),
            pltpu.VMEM((SIDE, SIDE), F32),
            pltpu.VMEM((ITERS + 1, SIDE, SIDE), F32),
            pltpu.VMEM((2, GROUP, SIDE, SIDE), BF16),
            pltpu.VMEM((2, NY, SIDE, SIDE), BF16),
            pltpu.VMEM((2, 2, 16, SIDE), F32),
            pltpu.VMEM((2, 2, 16, 16, SIDE), F32),
            pltpu.VMEM((8, SIDE), F32),
            pltpu.VMEM((8, 256), I32),
            pltpu.SMEM((8, 256), I32),
            pltpu.SemaphoreType.DMA((2,)),
            pltpu.SemaphoreType.DMA((2,)),
            pltpu.SemaphoreType.DMA((2, NZ)),
            pltpu.SemaphoreType.DMA((2, NZ, NX)),
            pltpu.SemaphoreType.DMA((2, NZ)),
            pltpu.SemaphoreType.DMA((2,)),
            pltpu.SemaphoreType.DMA((2, NY)),
            pltpu.SemaphoreType.DMA((2, 2)),
            pltpu.SemaphoreType.DMA((2, 2)),
        ],
        compiler_params=pltpu.CompilerParams(
            collective_id=0, has_side_effects=True, vmem_limit_bytes=56 * 1024 * 1024
        ),
        cost_estimate=pl.CostEstimate(flops=4_300_000_000, bytes_accessed=7_000_000, transcendentals=128),
        name="trust_step",
    )(y_prev, step_prev, accept, blk_row[0], blk_col[0], tiles)


def solution(mesh):
    placed = (
        P(("row", "col"), None),
        P(("row", "col"), None),
        P(("row", "col")),
        P("row", "col", None, None, None),
        P("row", "col", None),
        P("row", "col", None),
    )
    return jax.shard_map(
        shards,
        mesh=mesh,
        in_specs=placed,
        out_specs=(P(("row", "col"), None), P(("row", "col"), None)),
        check_vma=False,
    )
```

```python
import functools

import jax
import jax.numpy as jnp
from jax import lax
from jax.experimental import pallas as pl
from jax.experimental.pallas import tpu as pltpu
from jax.sharding import PartitionSpec as P

MESH = pl.DeviceIdType.MESH
ITERS = 3
DAMPING = 14.0
NZ, NX, NY = 8, 4, 4
SIDE = 128
GROUP = 4
TILES = 32
UPPER = 96
LOWER = SIDE - UPPER
Z_ORDER = (1, 7, 2, 6, 3, 5, 4)
LOW_ORDER = (1, 7, 2, 6, 3, 5, 4)
LATE = 1
X_ORDER = (2, 1, 3)
D_ORDER = (0,) + Z_ORDER
PAIRS = ((0, 0), (0, 1), (0, 2), (1, 1), (1, 2), (2, 2), (0, 3), (1, 3), (2, 3))
F32 = jnp.float32
BF16 = jnp.bfloat16
I32 = jnp.int32


def device(z, x, core, y):
    return ((z % NZ * NX + x % NX) * 2 + core % 2, y % NY)


def row_sum(a):
    return jnp.sum(a, axis=1, keepdims=True)


def slot_plan(rows, cols, z, x, core):
    slots = rows.shape[1]
    far = jnp.concatenate([rows, jnp.zeros((1, 256 - slots), I32)], axis=1)
    col = jnp.concatenate([cols, jnp.zeros((1, 256 - slots), I32)], axis=1)
    lane = lax.broadcasted_iota(I32, (1, 256), 1)
    dz = (z + NZ - col // 8) % NZ
    dx = (x + NX - (col // 2) % NX) % NX
    rel = (col + core) % 2
    key_row = jnp.where(lane < slots, ((rel * NZ + dz) * NX + dx) * GROUP + far, 1 << 12)
    sub2 = lax.broadcasted_iota(I32, (256, 256), 0)
    lane2 = lax.broadcasted_iota(I32, (256, 256), 1)
    key_r = jnp.broadcast_to(key_row, (256, 256))
    key_col = jnp.sum(jnp.where(sub2 == lane2, key_r, 0), axis=1, keepdims=True)
    key_c = jnp.broadcast_to(key_col, (256, 256))
    same_before = jnp.sum(jnp.where((key_r == key_c) & (lane2 < sub2), 1, 0), axis=1, keepdims=True)
    place = same_before + jnp.sum(jnp.where(key_r < key_c, 1, 0), axis=1, keepdims=True)
    here = jnp.broadcast_to(place, (256, 256)) == lane2
    order = jnp.sum(jnp.where(here, sub2, 0), axis=0, keepdims=True)
    keep = jnp.sum(jnp.where(here & (jnp.broadcast_to(same_before, (256, 256)) > 0), 1, 0), axis=0, keepdims=True)
    upto = jnp.sum(jnp.where(key_c <= lane2, 1, 0), axis=0, keepdims=True)
    found = jnp.sum(jnp.where(key_c == lane2, 1, 0), axis=0, keepdims=True)
    last = jnp.where(found > 0, upto - 1, slots)
    return jnp.concatenate([order, keep, last, jnp.zeros((5, 256), I32)], axis=0)


def kernel(
    slots, y_ref, step_ref, accept_ref, row_ref, col_ref, blocks_ref, out_step, out_res,
    raw, comp, dense, lent, gat, acc, acc_far, point, lam, vs, lean_rows, part, got, halves, ar_own, ar_buf, theta, plan_v, plan_s,
    local_sem, gs, zr, br, xr, lent_s, lent_r, ws, wr, ps, pr, hs, hr, ars, arr,
):
    row = lax.axis_index("row")
    y = lax.axis_index("col")
    z, x, core = row // (2 * NX), row // 2 % NX, row % 2

    first = [device(z + dz, x, core + dk, y) for dz in range(NZ) for dk in range(2)]
    second = [device(z, x + dx, core, y + dy) for dx in range(NX) for dy in range(NY)]
    owners = [device(z, x, core + j, y + dy) for j in range(2) for dy in range(NY)]
    peers = (first, second)
    greeted = first[1:] + second[1:] + owners[5:]

    barrier = pltpu.get_barrier_semaphore()
    for peer in greeted:
        pl.semaphore_signal(barrier, inc=1, device_id=peer, device_id_type=MESH)
    blocks_copy = pltpu.make_async_copy(blocks_ref, raw, local_sem.at[0])
    blocks_copy.start()

    moved = y_ref[...] + accept_ref[0].astype(F32) * step_ref[...]
    unit = moved * lax.rsqrt(row_sum(moved * moved) + 1e-06)
    point[...] = unit
    gat[0, 0] = unit.astype(BF16)
    vs[0] = jnp.zeros((SIDE, SIDE), F32)
    lam[...] = jnp.zeros((SIDE, SIDE), F32)
    theta[...] = jnp.zeros((8, SIDE), F32)
    out_res[...] = jnp.zeros((SIDE, SIDE), F32)
    plan_v[...] = slot_plan(row_ref[...], col_ref[...], z, x, core)
    plan_copy = pltpu.make_async_copy(plan_v, plan_s, local_sem.at[1])
    plan_copy.start()
    comp[slots] = jnp.zeros((SIDE, SIDE), BF16)
    pl.semaphore_wait(barrier, len(greeted))

    def remote(src, dst, send, recv, peer):
        return pltpu.make_async_remote_copy(
            src_ref=src, dst_ref=dst, send_sem=send, recv_sem=recv, device_id=peer, device_id_type=MESH
        )

    def settle(ref, sem):
        pltpu.make_async_copy(ref, ref, sem).wait()

    def reduce_send(use, stage):
        for j in range(1, 16):
            remote(
                ar_own.at[use, stage], ar_buf.at[use, stage, j], ars.at[use, stage], arr.at[use, stage], peers[stage][j]
            ).start()

    def reduce_take(use, stage):
        settle(ar_buf.at[use, stage, pl.ds(1, 15)], arr.at[use, stage])
        return ar_own[use, stage] + jnp.sum(ar_buf[use, stage, 1:16], axis=0)

    def compact(start, count):
        def one(j, total):
            total = plan_s[1, j].astype(F32) * total + raw[plan_s[0, j]].astype(F32)
            comp[j] = total.astype(BF16)
            return total

        out_res[...] = lax.fori_loop(start, start + count, one, out_res[...])

    def densify(chunk, store):
        def one(r, carry):
            store(
                pl.multiple_of(r * SIDE, SIDE),
                jnp.concatenate([comp[plan_s[2, chunk * 16 + i * GROUP + r]] for i in range(NX)], axis=1),
            )
            return carry

        lax.fori_loop(0, GROUP, one, 0)

    def lend(d):
        return remote(lent.at[d], dense.at[d, pl.ds(GROUP * SIDE, GROUP * SIDE)], lent_s, lent_r.at[d], owners[NY])

    def product(k, carry):
        p = k % 2

        def tile(d, dx):
            return gat.at[p, d * NX + dx, pl.ds(0, UPPER)]

        def low(d, dx, count):
            return gat.at[p, pl.ds(d * NX + dx, count), pl.ds(UPPER, LOWER)]

        def z_copy(d):
            return remote(tile(0, 0), tile(d, 0), gs.at[p], zr.at[p, d], device(z + d, x, core, y))

        def x_copy(d, dx):
            return remote(tile(d, 0), tile(d, dx), gs.at[p], xr.at[p, d], device(z, x + dx, core, y))

        def low_x_copy(dx):
            return remote(low(0, 0, 1), low(0, dx, 1), gs.at[p], br.at[p, dx], device(z, x + dx, core, y))

        def low_z_copy(d):
            return remote(low(0, 0, NX), low(d, 0, NX), gs.at[p], xr.at[p, d], device(z + d, x, core, y))

        def part_copy(o):
            return remote(part.at[p, (y + o) % NY], got.at[p, o], ps.at[p], pr.at[p], owners[o])

        def core_copy():
            return remote(halves.at[p, 0], halves.at[p, 1], hs.at[p], hr.at[p], owners[NY])

        def multiply(total, at, d, fresh):
            term = jnp.dot(
                dense[d, at : at + GROUP * SIDE],
                gat[p, d * NX : d * NX + NX].reshape(NX * SIDE, SIDE),
                preferred_element_type=F32,
            )
            total[...] = term if fresh else total[...] + term

        for d in Z_ORDER:
            z_copy(d).start()
        for dx in (1, 3, 2):
            low_x_copy(dx).start()
        for dx in X_ORDER:
            x_copy(0, dx).start()

        @pl.when(k >= 1)
        def _():
            settle(part.at[1 - p, pl.ds(0, 3)], ps.at[1 - p])
            settle(halves.at[1 - p, 0], hs.at[1 - p])
            for o in range(1, 8):
                remote(lean_rows.at[k - 1, 0], lean_rows.at[k - 1, o], ws.at[k - 1], wr.at[k - 1], owners[o]).start()

        @pl.when(k == 1)
        def _():
            reduce_send(0, 0)

        @pl.when(k == 0)
        def _():
            plan_copy.wait()
            blocks_copy.wait()
            compact(0, 24)

        for dx in (1, 3, 2):
            low_x_copy(dx).wait_recv()
        for d in LOW_ORDER:
            low_z_copy(d).start()
        for i, d in enumerate(Z_ORDER):

            @pl.when(k == 0)
            def _():
                compact(24 + 24 * i, 24)

            z_copy(d).wait_recv()
            for dx in X_ORDER:
                x_copy(d, dx).start()

        @pl.when(k == 1)
        def _():
            ar_own[0, 1] = reduce_take(0, 0)
            reduce_send(0, 1)

        @pl.when(k == 0)
        def _():
            for d in D_ORDER:

                def put(r, value):
                    lent[d, pl.ds(r, SIDE), :] = value

                densify(NZ + d, put)
                lend(d).start()
            for d in D_ORDER:

                def keep(r, value):
                    dense[d, pl.ds(r, SIDE), :] = value

                densify(d, keep)

        @pl.when(k == ITERS)
        def _():
            ar_own[1, 0] = local_grams()

        for i, d in enumerate(D_ORDER):
            rest = 3 * UPPER + (NX * LOWER if d else 0)
            settle(gat.at[p, pl.ds(0, rest // 32), pl.ds(0, 32)], xr.at[p, d])

            @pl.when(k == 0)
            def _():
                lend(d).wait_recv()

            multiply(acc_far, GROUP * SIDE, d, i == 0)
            if i < NZ - LATE:
                multiply(acc, 0, d, i == 0)

        for r in range(GROUP):
            halves[p, 0, r] = acc_far[r * SIDE : (r + 1) * SIDE, :].astype(BF16)
        core_copy().start()
        for d in D_ORDER[NZ - LATE :]:
            multiply(acc, 0, d, False)

        @pl.when(k == ITERS)
        def _():
            ar_own[1, 0] = ar_own[1, 0] + far_grams()
            reduce_send(1, 0)

        core_copy().wait_recv()
        for r in range(GROUP):
            both = acc[r * SIDE : (r + 1) * SIDE, :] + halves[p, 1, r].astype(F32)
            acc[r * SIDE : (r + 1) * SIDE, :] = both
            part[p, r] = both.astype(BF16)
        for o in (2, 1, 3):
            part_copy(o).start()
        settle(gat.at[p, pl.ds(0, 31)], gs.at[p])

        @pl.when(k == 1)
        def _():
            sums = reduce_take(0, 1)
            theta[...] = jnp.broadcast_to(DAMPING - sums[0:1] / sums[1:2], (8, SIDE))

        own = acc[pl.ds(pl.multiple_of(y * SIDE, SIDE), SIDE), :]
        settle(got.at[p, pl.ds(1, 3)], pr.at[p])
        for o in range(1, NY):
            own = own + got[p, o].astype(F32)
        full = 2.0 * own
        unit = point[...]
        lean = row_sum(unit * full)
        flat = full - lean * unit
        lam[...] = jnp.where(k == 0, jnp.broadcast_to(lean, (SIDE, SIDE)), lam[...])
        before = vs[jnp.maximum(k - 1, 0)]
        new = jnp.where(k == 0, -flat, flat + (DAMPING - theta[0:1, :] - lam[...]) * before)
        vs[k] = new
        gat[1 - p, 0] = new.astype(BF16)

        @pl.when(k < ITERS)
        def _():
            lean_rows[k, 0] = (new - row_sum(unit * new) * unit).astype(BF16)

        @pl.when(k == 0)
        def _():
            square = new * new
            ar_own[0, 0] = lane_sums([lam[...] * square, square])
            settle(lent, lent_s)

        return carry

    def lane_sums(terms):
        rows = [jnp.sum(term, axis=0, keepdims=True) for term in terms]
        rows.append(jnp.zeros((16 - len(rows), SIDE), F32))
        return jnp.broadcast_to(row_sum(jnp.concatenate(rows, axis=0)), (16, SIDE))

    def local_grams():
        pull = (DAMPING - theta[0:1, :] - lam[...]) * vs[2]
        return lane_sums([vs[i] * (vs[j] if j < ITERS else pull) for i, j in PAIRS])

    def far_grams():
        sums = [jnp.zeros((SIDE, SIDE), F32)] * ITERS
        for i in range(ITERS):
            settle(lean_rows.at[i, pl.ds(1, 7)], wr.at[i])
        for b in range(2 * GROUP):
            block = 2.0 * (acc, acc_far)[b // GROUP][b % GROUP * SIDE : (b % GROUP + 1) * SIDE, :]
            o = b // GROUP * NY + (y + NY - b % GROUP) % NY
            for i in range(ITERS):
                sums[i] = sums[i] + lean_rows[i, o].astype(F32) * block
        zero = jnp.zeros((SIDE, SIDE), F32)
        return lane_sums([zero if j < ITERS else sums[i] for i, j in PAIRS])

    lax.fori_loop(0, ITERS + 1, product, 0)

    ar_own[1, 1] = reduce_take(1, 0)
    reduce_send(1, 1)
    total = reduce_take(1, 1)
    gram = {pair: total[e : e + 1, :] for e, pair in enumerate(PAIRS)}
    shift = theta[0:1, :]

    def dot(a, b):
        terms = [a[i] * b[j] * gram[(min(i, j), max(i, j))] for i in a for j in b]
        return functools.reduce(lambda s, t: s + t, terms)

    def axpy(a, scale, b):
        out = dict(a)
        for i, v in b.items():
            out[i] = out[i] + scale * v if i in out else scale * v
        return out

    one = jnp.ones((1, SIDE), F32)
    residual = {0: one}
    direction = {0: one}
    step = {}
    norm_now = dot(residual, residual)
    for turn in range(ITERS):
        image = {i + 1: v for i, v in direction.items()}
        image = axpy(image, shift, direction)
        alpha = norm_now / dot(direction, image)
        step = axpy(step, alpha, direction)
        residual = axpy(residual, -alpha, image)
        if turn < ITERS - 1:
            norm_next = dot(residual, residual)
            direction = axpy(residual, norm_next / norm_now, direction)
            norm_now = norm_next
    out_step[...] = functools.reduce(lambda s, t: s + t, [step[i] * vs[i] for i in sorted(step)])
    out_res[...] = functools.reduce(lambda s, t: s + t, [residual[i] * vs[i] for i in sorted(residual)])

    settle(part.at[1, pl.ds(0, 3)], ps.at[1])
    settle(halves.at[1, 0], hs.at[1])
    for i in range(ITERS):
        settle(lean_rows.at[i, pl.ds(1, 7)], ws.at[i])
    for use in range(2):
        for stage in range(2):
            settle(ar_buf.at[use, stage, pl.ds(1, 15)], ars.at[use, stage])


def shards(y_prev, step_prev, accept, blocks, blk_row, blk_col):
    tiles = blocks[0, 0]
    slots = tiles.shape[0]
    vmem = pl.BlockSpec(memory_space=pltpu.VMEM)
    return pl.pallas_call(
        functools.partial(kernel, slots),
        out_shape=[jax.ShapeDtypeStruct(y_prev.shape, F32)] * 2,
        in_specs=[vmem, vmem, pl.BlockSpec(memory_space=pltpu.SMEM), vmem, vmem, pl.BlockSpec(memory_space=pl.ANY)],
        out_specs=[vmem, vmem],
        scratch_shapes=[
            pltpu.VMEM((slots, SIDE, SIDE), BF16),
            pltpu.VMEM((slots + 1, SIDE, SIDE), BF16),
            pltpu.VMEM((NZ, 2 * GROUP * SIDE, NX * SIDE), BF16),
            pltpu.VMEM((NZ, GROUP * SIDE, NX * SIDE), BF16),
            pltpu.VMEM((2, TILES, SIDE, SIDE), BF16),
            pltpu.VMEM((GROUP * SIDE, SIDE), F32),
            pltpu.VMEM((GROUP * SIDE, SIDE), F32),
            pltpu.VMEM((SIDE, SIDE), F32),
            pltpu.VMEM((SIDE, SIDE), F32),
            pltpu.VMEM((ITERS + 1, SIDE, SIDE), F32),
            pltpu.VMEM((ITERS, 2 * NY, SIDE, SIDE), BF16),
            pltpu.VMEM((2, GROUP, SIDE, SIDE), BF16),
            pltpu.VMEM((2, NY, SIDE, SIDE), BF16),
            pltpu.VMEM((2, 2, GROUP, SIDE, SIDE), BF16),
            pltpu.VMEM((2, 2, 16, SIDE), F32),
            pltpu.VMEM((2, 2, 16, 16, SIDE), F32),
            pltpu.VMEM((8, SIDE), F32),
            pltpu.VMEM((8, 256), I32),
            pltpu.SMEM((8, 256), I32),
            pltpu.SemaphoreType.DMA((2,)),
            pltpu.SemaphoreType.DMA((2,)),
            pltpu.SemaphoreType.DMA((2, NZ)),
            pltpu.SemaphoreType.DMA((2, NX)),
            pltpu.SemaphoreType.DMA((2, NZ)),
            pltpu.SemaphoreType.DMA,
            pltpu.SemaphoreType.DMA((NZ,)),
            pltpu.SemaphoreType.DMA((ITERS,)),
            pltpu.SemaphoreType.DMA((ITERS,)),
            pltpu.SemaphoreType.DMA((2,)),
            pltpu.SemaphoreType.DMA((2,)),
            pltpu.SemaphoreType.DMA((2,)),
            pltpu.SemaphoreType.DMA((2,)),
            pltpu.SemaphoreType.DMA((2, 2)),
            pltpu.SemaphoreType.DMA((2, 2)),
        ],
        compiler_params=pltpu.CompilerParams(
            collective_id=0, has_side_effects=True, vmem_limit_bytes=56 * 1024 * 1024
        ),
        cost_estimate=pl.CostEstimate(flops=4_300_000_000, bytes_accessed=7_000_000, transcendentals=128),
        name="trust_step",
    )(y_prev, step_prev, accept, blk_row[0], blk_col[0], tiles)


def solution(mesh):
    placed = (
        P(("row", "col"), None),
        P(("row", "col"), None),
        P(("row", "col")),
        P("row", "col", None, None, None),
        P("row", "col", None),
        P("row", "col", None),
    )
    return jax.shard_map(
        shards,
        mesh=mesh,
        in_specs=placed,
        out_specs=(P(("row", "col"), None), P(("row", "col"), None)),
        check_vma=False,
    )
```

```python
import functools

import jax
import jax.numpy as jnp
from jax import lax
from jax.experimental import pallas as pl
from jax.experimental.pallas import tpu as pltpu
from jax.sharding import PartitionSpec as P

MESH = pl.DeviceIdType.MESH
ITERS = 3
DAMPING = 14.0
NZ, NX, NY = 8, 4, 4
SIDE = 128
GROUP = 4
TILES = 32
UPPER = 96
LOWER = SIDE - UPPER
PLANES = (0, 1, 7, 2, 6, 3, 5, 4)
RUNS = ((1, 2), (3, 2), (5, 2), (7, 1))
X_ORDER = (2, 1, 3)
PAIRS = ((0, 0), (0, 1), (0, 2), (1, 1), (1, 2), (2, 2), (0, 3), (1, 3), (2, 3))
F32 = jnp.float32
BF16 = jnp.bfloat16
I32 = jnp.int32


def device(z, x, core, y):
    return ((z % NZ * NX + x % NX) * 2 + core % 2, y % NY)


def row_sum(a):
    return jnp.sum(a, axis=1, keepdims=True)


def slot_plan(rows, cols, z, x, core):
    slots = rows.shape[1]
    far = jnp.concatenate([rows, jnp.zeros((1, 256 - slots), I32)], axis=1)
    col = jnp.concatenate([cols, jnp.zeros((1, 256 - slots), I32)], axis=1)
    lane = lax.broadcasted_iota(I32, (1, 256), 1)
    dz = (z + NZ - col // 8) % NZ
    dz = jnp.where(dz == 0, 0, jnp.where(dz <= NZ // 2, 2 * dz - 1, 2 * (NZ - dz)))
    dx = (x + NX - (col // 2) % NX) % NX
    rel = (col + core) % 2
    key_row = jnp.where(lane < slots, ((rel * NZ + dz) * NX + dx) * GROUP + far, 1 << 12)
    sub2 = lax.broadcasted_iota(I32, (256, 256), 0)
    lane2 = lax.broadcasted_iota(I32, (256, 256), 1)
    key_r = jnp.broadcast_to(key_row, (256, 256))
    key_col = jnp.sum(jnp.where(sub2 == lane2, key_r, 0), axis=1, keepdims=True)
    key_c = jnp.broadcast_to(key_col, (256, 256))
    same_before = jnp.sum(jnp.where((key_r == key_c) & (lane2 < sub2), 1, 0), axis=1, keepdims=True)
    place = same_before + jnp.sum(jnp.where(key_r < key_c, 1, 0), axis=1, keepdims=True)
    here = jnp.broadcast_to(place, (256, 256)) == lane2
    order = jnp.sum(jnp.where(here, sub2, 0), axis=0, keepdims=True)
    keep = jnp.sum(jnp.where(here & (jnp.broadcast_to(same_before, (256, 256)) > 0), 1, 0), axis=0, keepdims=True)
    upto = jnp.sum(jnp.where(key_c <= lane2, 1, 0), axis=0, keepdims=True)
    found = jnp.sum(jnp.where(key_c == lane2, 1, 0), axis=0, keepdims=True)
    last = jnp.where(found > 0, upto - 1, slots)
    return jnp.concatenate([order, keep, last, jnp.zeros((5, 256), I32)], axis=0)


def kernel(
    slots, y_ref, step_ref, accept_ref, row_ref, col_ref, blocks_ref, out_step, out_res,
    raw, comp, dense, lent, arrivals, gat, acc, acc_far, point, lam, vs, lean_rows, part, got, halves, ar_own, ar_buf, theta, plan_v, plan_s,
    local_sem, gs, zr, br, xr, lent_s, lent_r, ws, wr, ps, pr, hs, hr, ars, arr,
):
    row = lax.axis_index("row")
    y = lax.axis_index("col")
    z, x, core = row // (2 * NX), row // 2 % NX, row % 2

    plane = [device(z + dz, x + dx, core, y) for dz in range(NZ) for dx in range(NX)]
    owners = [device(z, x, core + j, y + dy) for j in range(2) for dy in range(NY)]
    peers = (plane, owners)
    far_first = [
        sorted(range(1, m * n), key=lambda j: -(min(j // n, m - j // n) + min(j % n, n - j % n)))
        for m, n in ((NZ, NX), (2, NY))
    ]
    greeted = plane[1:] + owners[1:]

    barrier = pltpu.get_barrier_semaphore()
    for peer in greeted:
        pl.semaphore_signal(barrier, inc=1, device_id=peer, device_id_type=MESH)
    blocks_copy = pltpu.make_async_copy(blocks_ref, raw, local_sem.at[0])
    blocks_copy.start()

    moved = y_ref[...] + accept_ref[0].astype(F32) * step_ref[...]
    unit = moved * lax.rsqrt(row_sum(moved * moved) + 1e-06)
    point[...] = unit
    gat[0, 0, 0] = unit.astype(BF16)
    vs[0] = jnp.zeros((SIDE, SIDE), F32)
    lam[...] = jnp.zeros((SIDE, SIDE), F32)
    theta[...] = jnp.zeros((8, SIDE), F32)
    out_res[...] = jnp.zeros((SIDE, SIDE), F32)
    plan_copy = pltpu.make_async_copy(plan_v, plan_s, local_sem.at[1])
    comp[slots] = jnp.zeros((SIDE, SIDE), BF16)
    pl.semaphore_wait(barrier, len(greeted))

    diagonal = lax.broadcasted_iota(I32, (16, SIDE), 0) == lax.broadcasted_iota(I32, (16, SIDE), 1)

    def remote(src, dst, send, recv, peer):
        return pltpu.make_async_remote_copy(
            src_ref=src, dst_ref=dst, send_sem=send, recv_sem=recv, device_id=peer, device_id_type=MESH
        )

    def settle(ref, sem):
        pltpu.make_async_copy(ref, ref, sem).wait()

    def reduce_send(use, stage):
        for j in far_first[stage]:
            remote(
                ar_own.at[use, stage], ar_buf.at[use, stage, j], ars.at[use, stage], arr.at[use, stage], peers[stage][j]
            ).start()

    def reduce_take(use, stage):
        count = len(peers[stage])
        settle(ar_buf.at[use, stage, pl.ds(1, count - 1)], arr.at[use, stage])
        return ar_own[use, stage] + jnp.sum(ar_buf[use, stage, 1:count], axis=0)

    def spread(total):
        return jnp.broadcast_to(row_sum(jnp.where(diagonal, jnp.broadcast_to(total, (16, SIDE)), 0.0)), (16, SIDE))

    def compact(start, count):
        def one(j, total):
            total = plan_s[1, j].astype(F32) * total + raw[plan_s[0, j]].astype(F32)
            comp[j] = total.astype(BF16)
            return total

        out_res[...] = lax.fori_loop(start, start + count, one, out_res[...])

    def densify(chunk, store):
        def one(r, carry):
            store(
                pl.multiple_of(r * SIDE, SIDE),
                jnp.concatenate([comp[plan_s[2, chunk * 16 + i * GROUP + r]] for i in range(NX)], axis=1),
            )
            return carry

        lax.fori_loop(0, GROUP, one, 0)

    def lend(d):
        return remote(lent.at[d], dense.at[d, pl.ds(GROUP * SIDE, GROUP * SIDE)], lent_s, lent_r.at[d], owners[NY])

    def product(k, carry):
        p = k % 2

        def high(i, count, dx):
            return gat.at[p, pl.ds(i, count), dx, pl.ds(0, UPPER)]

        def low(i, dx, count):
            return gat.at[p, i, pl.ds(dx, count), pl.ds(UPPER, LOWER)]

        def z_copy(i):
            return remote(high(0, 1, 0), high(i, 1, 0), gs.at[p], zr.at[p, i], device(z + PLANES[i], x, core, y))

        def x_copy(i, count, dx):
            return remote(high(i, count, 0), high(i, count, dx), gs.at[p], xr.at[p, i], device(z, x + dx, core, y))

        def low_x_copy(dx):
            return remote(low(0, 0, 1), low(0, dx, 1), gs.at[p], br.at[p, dx], device(z, x + dx, core, y))

        def low_z_copy(i, run):
            return remote(low(0, 0, NX), low(i, 0, NX), gs.at[p], xr.at[p, run], device(z + PLANES[i], x, core, y))

        def part_copy(o):
            return remote(part.at[p, (y + o) % NY], got.at[p, o], ps.at[p], pr.at[p], owners[o])

        def core_copy(dy):
            r = (y + dy) % NY
            return remote(halves.at[p, 0, r], halves.at[p, 1, r], hs.at[p], hr.at[p, dy], owners[NY])

        def multiply(total, at, i, count):
            term = functools.reduce(
                lambda s, t: s + t,
                [
                    jnp.dot(
                        dense[n, at : at + GROUP * SIDE],
                        gat[p, n].reshape(NX * SIDE, SIDE),
                        preferred_element_type=F32,
                    )
                    for n in range(i, i + count)
                ],
            )
            total[...] = total[...] + term if i else term

        for i in range(1, NZ):
            z_copy(i).start()
        for dx in (1, 3, 2):
            low_x_copy(dx).start()
        for dx in X_ORDER:
            x_copy(0, 1, dx).start()

        @pl.when(k >= 1)
        def _():
            settle(part.at[1 - p, pl.ds(0, 3)], ps.at[1 - p])
            settle(halves.at[1 - p, 0], hs.at[1 - p])
            new = vs[k - 1]
            lean_rows[k - 1, 0] = (new - row_sum(point[...] * new) * point[...]).astype(BF16)

        @pl.when(k == 1)
        def _():
            square = vs[0] * vs[0]
            ar_own[0, 0] = lane_sums([lam[...] * square, square])
            reduce_send(0, 0)

        @pl.when(k == 0)
        def _():
            plan_v[...] = slot_plan(row_ref[...], col_ref[...], z, x, core)
            plan_copy.start()

        for dx in (1, 3, 2):
            low_x_copy(dx).wait_recv()

        @pl.when(k == 0)
        def _():
            plan_copy.wait()
            blocks_copy.wait()

        for n, (i, count) in enumerate(RUNS):

            @pl.when(k == 0)
            def _():
                compact(48 * n, 48)

            for m in range(count):
                z_copy(i + m).wait_recv()
            for dx in X_ORDER:
                x_copy(i, count, dx).start()
            if n == 0:
                for m in range(1, NZ):
                    low_z_copy(m, next(i0 for i0, c in RUNS if i0 <= m < i0 + c)).start()

        @pl.when(k >= 1)
        def _():
            for o in range(1, 8):
                remote(lean_rows.at[k - 1, 0], lean_rows.at[k - 1, o], ws.at[k - 1], wr.at[k - 1], owners[o]).start()

        @pl.when(k == 1)
        def _():
            ar_own[0, 1] = reduce_take(0, 0)
            reduce_send(0, 1)

        @pl.when(k == 0)
        def _():
            for i in range(NZ):

                def put(r, value):
                    lent[i, pl.ds(r, SIDE), :] = value

                densify(NZ + i, put)
                lend(i).start()
            for i in range(NZ):

                def keep(r, value):
                    dense[i, pl.ds(r, SIDE), :] = value

                densify(i, keep)

        @pl.when(k == ITERS)
        def _():
            ar_own[1, 0] = local_grams()

        for i, count in ((0, 1),) + RUNS:
            rest = count * (3 * UPPER + (NX * LOWER if i else 0)) // 32
            settle(arrivals.at[pl.ds(0, rest)], xr.at[p, i])

            @pl.when(k == 0)
            def _():
                for n in range(i, i + count):
                    lend(n).wait_recv()

            multiply(acc_far, GROUP * SIDE, i, count)
            if i != RUNS[-1][0]:
                multiply(acc, 0, i, count)

        for dy in (2, 1, 3, 0):
            r = (y + dy) % NY
            halves[p, 0, r] = acc_far[pl.ds(pl.multiple_of(r * SIDE, SIDE), SIDE), :].astype(BF16)
            core_copy(dy).start()
        multiply(acc, 0, *RUNS[-1])

        @pl.when(k == ITERS)
        def _():
            ar_own[1, 0] = ar_own[1, 0] + far_grams()
            reduce_send(1, 0)

        for dy in (2, 1, 3):
            core_copy(dy).wait_recv()
            r = (y + dy) % NY
            both = acc[pl.ds(pl.multiple_of(r * SIDE, SIDE), SIDE), :] + halves[p, 1, r].astype(F32)
            part[p, r] = both.astype(BF16)
            part_copy(dy).start()
        core_copy(0).wait_recv()
        settle(arrivals.at[pl.ds(0, 31 * NX)], gs.at[p])

        @pl.when(k == 1)
        def _():
            sums = spread(reduce_take(0, 1))
            theta[...] = jnp.broadcast_to(DAMPING - sums[0:1] / sums[1:2], (8, SIDE))

        own = acc[pl.ds(pl.multiple_of(y * SIDE, SIDE), SIDE), :] + halves[p, 1, y].astype(F32)
        settle(got.at[p, pl.ds(1, 3)], pr.at[p])
        for o in range(1, NY):
            own = own + got[p, o].astype(F32)
        full = 2.0 * own
        unit = point[...]
        lean = row_sum(unit * full)
        flat = full - lean * unit
        lam[...] = jnp.where(k == 0, jnp.broadcast_to(lean, (SIDE, SIDE)), lam[...])
        before = vs[jnp.maximum(k - 1, 0)]
        new = jnp.where(k == 0, -flat, flat + (DAMPING - theta[0:1, :] - lam[...]) * before)
        vs[k] = new
        gat[1 - p, 0, 0] = new.astype(BF16)

        @pl.when(k == 0)
        def _():
            settle(lent, lent_s)

        return carry

    def lane_sums(terms):
        rows = [jnp.sum(term, axis=0, keepdims=True) for term in terms]
        rows.append(jnp.zeros((16 - len(rows), SIDE), F32))
        sums = jnp.broadcast_to(row_sum(jnp.concatenate(rows, axis=0)), (16, SIDE))
        return jnp.sum(jnp.where(diagonal, sums, 0.0), axis=0, keepdims=True)

    def local_grams():
        pull = (DAMPING - theta[0:1, :] - lam[...]) * vs[2]
        return lane_sums([vs[i] * (vs[j] if j < ITERS else pull) for i, j in PAIRS])

    def far_grams():
        sums = [jnp.zeros((SIDE, SIDE), F32)] * ITERS
        for i in range(ITERS):
            settle(lean_rows.at[i, pl.ds(1, 7)], wr.at[i])
        for b in range(2 * GROUP):
            block = 2.0 * (acc, acc_far)[b // GROUP][b % GROUP * SIDE : (b % GROUP + 1) * SIDE, :]
            o = b // GROUP * NY + (y + NY - b % GROUP) % NY
            for i in range(ITERS):
                sums[i] = sums[i] + lean_rows[i, o].astype(F32) * block
        zero = jnp.zeros((SIDE, SIDE), F32)
        return lane_sums([zero if j < ITERS else sums[i] for i, j in PAIRS])

    lax.fori_loop(0, ITERS + 1, product, 0)

    ar_own[1, 1] = reduce_take(1, 0)
    reduce_send(1, 1)
    total = spread(reduce_take(1, 1))
    gram = {pair: total[e : e + 1, :] for e, pair in enumerate(PAIRS)}
    shift = theta[0:1, :]

    def dot(a, b):
        terms = [a[i] * b[j] * gram[(min(i, j), max(i, j))] for i in a for j in b]
        return functools.reduce(lambda s, t: s + t, terms)

    def axpy(a, scale, b):
        out = dict(a)
        for i, v in b.items():
            out[i] = out[i] + scale * v if i in out else scale * v
        return out

    one = jnp.ones((1, SIDE), F32)
    residual = {0: one}
    direction = {0: one}
    step = {}
    norm_now = dot(residual, residual)
    for turn in range(ITERS):
        image = {i + 1: v for i, v in direction.items()}
        image = axpy(image, shift, direction)
        alpha = norm_now / dot(direction, image)
        step = axpy(step, alpha, direction)
        residual = axpy(residual, -alpha, image)
        if turn < ITERS - 1:
            norm_next = dot(residual, residual)
            direction = axpy(residual, norm_next / norm_now, direction)
            norm_now = norm_next
    out_step[...] = functools.reduce(lambda s, t: s + t, [step[i] * vs[i] for i in sorted(step)])
    out_res[...] = functools.reduce(lambda s, t: s + t, [residual[i] * vs[i] for i in sorted(residual)])

    settle(part.at[1, pl.ds(0, 3)], ps.at[1])
    settle(halves.at[1, 0], hs.at[1])
    for i in range(ITERS):
        settle(lean_rows.at[i, pl.ds(1, 7)], ws.at[i])
    for use in range(2):
        for stage in range(2):
            settle(ar_buf.at[use, stage, pl.ds(1, len(peers[stage]) - 1)], ars.at[use, stage])


def finish(step_ref, res_ref, out_step, out_res):
    out_step[...] = step_ref[...]
    out_res[...] = res_ref[...]


def shards(y_prev, step_prev, accept, blocks, blk_row, blk_col):
    tiles = blocks[0, 0]
    slots = tiles.shape[0]
    vmem = pl.BlockSpec(memory_space=pltpu.VMEM)
    both = pl.pallas_call(
        functools.partial(kernel, slots),
        out_shape=[jax.ShapeDtypeStruct(y_prev.shape, F32)] * 2,
        in_specs=[vmem, vmem, pl.BlockSpec(memory_space=pltpu.SMEM), vmem, vmem, pl.BlockSpec(memory_space=pl.ANY)],
        out_specs=[vmem, vmem],
        scratch_shapes=[
            pltpu.VMEM((slots, SIDE, SIDE), BF16),
            pltpu.VMEM((slots + 1, SIDE, SIDE), BF16),
            pltpu.VMEM((NZ, 2 * GROUP * SIDE, NX * SIDE), BF16),
            pltpu.VMEM((NZ, GROUP * SIDE, NX * SIDE), BF16),
            pltpu.VMEM((TILES * NX, SIDE // NX, SIDE), BF16),
            pltpu.VMEM((2, NZ, NX, SIDE, SIDE), BF16),
            pltpu.VMEM((GROUP * SIDE, SIDE), F32),
            pltpu.VMEM((GROUP * SIDE, SIDE), F32),
            pltpu.VMEM((SIDE, SIDE), F32),
            pltpu.VMEM((SIDE, SIDE), F32),
            pltpu.VMEM((ITERS + 1, SIDE, SIDE), F32),
            pltpu.VMEM((ITERS, 2 * NY, SIDE, SIDE), BF16),
            pltpu.VMEM((2, GROUP, SIDE, SIDE), BF16),
            pltpu.VMEM((2, NY, SIDE, SIDE), BF16),
            pltpu.VMEM((2, 2, GROUP, SIDE, SIDE), BF16),
            pltpu.VMEM((2, 2, 1, SIDE), F32),
            pltpu.VMEM((2, 2, NZ * NX, 1, SIDE), F32),
            pltpu.VMEM((8, SIDE), F32),
            pltpu.VMEM((8, 256), I32),
            pltpu.SMEM((8, 256), I32),
            pltpu.SemaphoreType.DMA((2,)),
            pltpu.SemaphoreType.DMA((2,)),
            pltpu.SemaphoreType.DMA((2, NZ)),
            pltpu.SemaphoreType.DMA((2, NX)),
            pltpu.SemaphoreType.DMA((2, NZ)),
            pltpu.SemaphoreType.DMA,
            pltpu.SemaphoreType.DMA((NZ,)),
            pltpu.SemaphoreType.DMA((ITERS,)),
            pltpu.SemaphoreType.DMA((ITERS,)),
            pltpu.SemaphoreType.DMA((2,)),
            pltpu.SemaphoreType.DMA((2,)),
            pltpu.SemaphoreType.DMA((2,)),
            pltpu.SemaphoreType.DMA((2, NY)),
            pltpu.SemaphoreType.DMA((2, 2)),
            pltpu.SemaphoreType.DMA((2, 2)),
        ],
        compiler_params=pltpu.CompilerParams(
            collective_id=0, has_side_effects=True, vmem_limit_bytes=56 * 1024 * 1024
        ),
        cost_estimate=pl.CostEstimate(flops=4_300_000_000, bytes_accessed=7_000_000, transcendentals=128),
        name="trust_step",
    )(y_prev, step_prev, accept, blk_row[0], blk_col[0], tiles)
    return pl.pallas_call(
        finish,
        out_shape=[jax.ShapeDtypeStruct(y_prev.shape, F32)] * 2,
        in_specs=[vmem, vmem],
        out_specs=[vmem, vmem],
        name="finish",
    )(*both)


def solution(mesh):
    placed = (
        P(("row", "col"), None),
        P(("row", "col"), None),
        P(("row", "col")),
        P("row", "col", None, None, None),
        P("row", "col", None),
        P("row", "col", None),
    )
    return jax.shard_map(
        shards,
        mesh=mesh,
        in_specs=placed,
        out_specs=(P(("row", "col"), None), P(("row", "col"), None)),
        check_vma=False,
    )
```

```python
import functools

import jax
import jax.numpy as jnp
from jax import lax
from jax.experimental import pallas as pl
from jax.experimental.pallas import tpu as pltpu
from jax.sharding import PartitionSpec as P

MESH = pl.DeviceIdType.MESH
ITERS = 3
DAMPING = 14.0
NZ, NX, NY = 8, 4, 4
SIDE = 128
GROUP = 4
TILES = 32
UPPER = 96
LOWER = SIDE - UPPER
PLANES = (0, 1, 7, 2, 6, 3, 5, 4)
RUNS = ((1, 2), (3, 2), (5, 2), (7, 1))
X_ORDER = (2, 1, 3)
PAIRS = ((0, 0), (0, 1), (0, 2), (1, 1), (1, 2), (2, 2), (0, 3), (1, 3), (2, 3))
F32 = jnp.float32
BF16 = jnp.bfloat16
I32 = jnp.int32


def device(z, x, core, y):
    return ((z % NZ * NX + x % NX) * 2 + core % 2, y % NY)


def row_sum(a):
    return jnp.sum(a, axis=1, keepdims=True)


def slot_plan(rows, cols, z, x, core):
    slots = rows.shape[1]
    far = jnp.concatenate([rows, jnp.zeros((1, 256 - slots), I32)], axis=1)
    col = jnp.concatenate([cols, jnp.zeros((1, 256 - slots), I32)], axis=1)
    lane = lax.broadcasted_iota(I32, (1, 256), 1)
    dz = (z + NZ - col // 8) % NZ
    dz = jnp.where(dz == 0, 0, jnp.where(dz <= NZ // 2, 2 * dz - 1, 2 * (NZ - dz)))
    dx = (x + NX - (col // 2) % NX) % NX
    rel = (col + core) % 2
    key_row = jnp.where(lane < slots, ((rel * NZ + dz) * NX + dx) * GROUP + far, 1 << 12)
    sub2 = lax.broadcasted_iota(I32, (256, 256), 0)
    lane2 = lax.broadcasted_iota(I32, (256, 256), 1)
    key_r = jnp.broadcast_to(key_row, (256, 256))
    key_col = jnp.sum(jnp.where(sub2 == lane2, key_r, 0), axis=1, keepdims=True)
    key_c = jnp.broadcast_to(key_col, (256, 256))
    same_before = jnp.sum(jnp.where((key_r == key_c) & (lane2 < sub2), 1, 0), axis=1, keepdims=True)
    place = same_before + jnp.sum(jnp.where(key_r < key_c, 1, 0), axis=1, keepdims=True)
    here = jnp.broadcast_to(place, (256, 256)) == lane2
    order = jnp.sum(jnp.where(here, sub2, 0), axis=0, keepdims=True)
    keep = jnp.sum(jnp.where(here & (jnp.broadcast_to(same_before, (256, 256)) > 0), 1, 0), axis=0, keepdims=True)
    upto = jnp.sum(jnp.where(key_c <= lane2, 1, 0), axis=0, keepdims=True)
    found = jnp.sum(jnp.where(key_c == lane2, 1, 0), axis=0, keepdims=True)
    last = jnp.where(found > 0, upto - 1, slots)
    return jnp.concatenate([order, keep, last, jnp.zeros((5, 256), I32)], axis=0)


def kernel(
    slots, y_hbm, step_hbm, accept_hbm, row_hbm, col_hbm, blocks_ref, out_step, out_res,
    y_ref, step_ref, accept_ref, row_ref, col_ref, raw, comp, dense, lent, arrivals, gat, acc, acc_far, point, lam, vs, lean_rows, part, got, halves, ar_own, ar_buf, theta, plan_v, plan_s,
    local_sem, gs, zr, br, xr, lent_s, lent_r, ws, wr, ps, pr, hs, hr, ars, arr,
):
    row = lax.axis_index("row")
    y = lax.axis_index("col")
    z, x, core = row // (2 * NX), row // 2 % NX, row % 2

    plane = [device(z + dz, x + dx, core, y) for dz in range(NZ) for dx in range(NX)]
    owners = [device(z, x, core + j, y + dy) for j in range(2) for dy in range(NY)]
    peers = (plane, owners)
    far_first = [
        sorted(range(1, m * n), key=lambda j: -(min(j // n, m - j // n) + min(j % n, n - j % n)))
        for m, n in ((NZ, NX), (2, NY))
    ]
    greeted = plane[1:NX] + plane[NX::NX] + owners[1:]

    barrier = pltpu.get_barrier_semaphore()
    for peer in greeted:
        pl.semaphore_signal(barrier, inc=1, device_id=peer, device_id_type=MESH)
    pairs = ((y_hbm, y_ref), (step_hbm, step_ref), (accept_hbm, accept_ref), (row_hbm, row_ref), (col_hbm, col_ref))
    small = [pltpu.make_async_copy(src, dst, local_sem.at[2 + n]) for n, (src, dst) in enumerate(pairs)]
    for copy in small:
        copy.start()
    blocks_copy = pltpu.make_async_copy(blocks_ref, raw, local_sem.at[0])
    blocks_copy.start()
    for copy in small:
        copy.wait()

    moved = y_ref[...] + accept_ref[...].astype(F32) * step_ref[...]
    unit = moved * lax.rsqrt(row_sum(moved * moved) + 1e-06)
    point[...] = unit
    gat[0, 0, 0] = unit.astype(BF16)
    vs[0] = jnp.zeros((SIDE, SIDE), F32)
    lam[...] = jnp.zeros((SIDE, SIDE), F32)
    theta[...] = jnp.zeros((8, SIDE), F32)
    out_res[...] = jnp.zeros((SIDE, SIDE), F32)
    plan_copy = pltpu.make_async_copy(plan_v, plan_s, local_sem.at[1])
    comp[slots] = jnp.zeros((SIDE, SIDE), BF16)
    pl.semaphore_wait(barrier, len(greeted))

    diagonal = lax.broadcasted_iota(I32, (16, SIDE), 0) == lax.broadcasted_iota(I32, (16, SIDE), 1)

    def remote(src, dst, send, recv, peer):
        return pltpu.make_async_remote_copy(
            src_ref=src, dst_ref=dst, send_sem=send, recv_sem=recv, device_id=peer, device_id_type=MESH
        )

    def settle(ref, sem):
        pltpu.make_async_copy(ref, ref, sem).wait()

    def reduce_send(use, stage):
        for j in far_first[stage]:
            remote(
                ar_own.at[use, stage], ar_buf.at[use, stage, j], ars.at[use, stage], arr.at[use, stage], peers[stage][j]
            ).start()

    def reduce_take(use, stage):
        count = len(peers[stage])
        settle(ar_buf.at[use, stage, pl.ds(1, count - 1)], arr.at[use, stage])
        return ar_own[use, stage] + jnp.sum(ar_buf[use, stage, 1:count], axis=0)

    def spread(total):
        return jnp.broadcast_to(row_sum(jnp.where(diagonal, jnp.broadcast_to(total, (16, SIDE)), 0.0)), (16, SIDE))

    def compact(start, count):
        def one(j, total):
            total = plan_s[1, j].astype(F32) * total + raw[plan_s[0, j]].astype(F32)
            comp[j] = total.astype(BF16)
            return total

        out_res[...] = lax.fori_loop(start, start + count, one, out_res[...])

    def densify(chunk, store):
        def one(r, carry):
            store(
                pl.multiple_of(r * SIDE, SIDE),
                jnp.concatenate([comp[plan_s[2, chunk * 16 + i * GROUP + r]] for i in range(NX)], axis=1),
            )
            return carry

        lax.fori_loop(0, GROUP, one, 0)

    def lend(d):
        return remote(lent.at[d], dense.at[d, pl.ds(GROUP * SIDE, GROUP * SIDE)], lent_s, lent_r.at[d], owners[NY])

    def product(k, carry):
        p = k % 2

        def high(i, count, dx):
            return gat.at[p, pl.ds(i, count), dx, pl.ds(0, UPPER)]

        def low(i, dx, count):
            return gat.at[p, i, pl.ds(dx, count), pl.ds(UPPER, LOWER)]

        def z_copy(i):
            return remote(high(0, 1, 0), high(i, 1, 0), gs.at[p], zr.at[p, i], device(z + PLANES[i], x, core, y))

        def x_copy(i, count, dx):
            return remote(high(i, count, 0), high(i, count, dx), gs.at[p], xr.at[p, i], device(z, x + dx, core, y))

        def low_x_copy(dx):
            return remote(low(0, 0, 1), low(0, dx, 1), gs.at[p], br.at[p, dx], device(z, x + dx, core, y))

        def low_z_copy(i, run):
            return remote(low(0, 0, NX), low(i, 0, NX), gs.at[p], xr.at[p, run], device(z + PLANES[i], x, core, y))

        def part_copy(o):
            return remote(part.at[p, (y + o) % NY], got.at[p, o], ps.at[p], pr.at[p], owners[o])

        def core_copy(dy):
            r = (y + dy) % NY
            return remote(halves.at[p, 0, r], halves.at[p, 1, r], hs.at[p], hr.at[p, dy], owners[NY])

        def multiply(total, at, i, count):
            term = functools.reduce(
                lambda s, t: s + t,
                [
                    jnp.dot(
                        dense[n, at : at + GROUP * SIDE],
                        gat[p, n].reshape(NX * SIDE, SIDE),
                        preferred_element_type=F32,
                    )
                    for n in range(i, i + count)
                ],
            )
            total[...] = total[...] + term if i else term

        for i in range(1, NZ):
            z_copy(i).start()
        for dx in (1, 3, 2):
            low_x_copy(dx).start()
        for dx in X_ORDER:
            x_copy(0, 1, dx).start()

        @pl.when(k >= 1)
        def _():
            settle(part.at[1 - p, pl.ds(0, 3)], ps.at[1 - p])
            settle(halves.at[1 - p, 0], hs.at[1 - p])
            new = vs[k - 1]
            lean_rows[k - 1, 0] = (new - row_sum(point[...] * new) * point[...]).astype(BF16)

        @pl.when(k == 1)
        def _():
            square = vs[0] * vs[0]
            ar_own[0, 0] = lane_sums([lam[...] * square, square])
            reduce_send(0, 0)

        @pl.when(k == 0)
        def _():
            plan_v[...] = slot_plan(row_ref[...], col_ref[...], z, x, core)
            plan_copy.start()

        for dx in (1, 3, 2):
            low_x_copy(dx).wait_recv()

        @pl.when(k == 0)
        def _():
            plan_copy.wait()
            blocks_copy.wait()

        for n, (i, count) in enumerate(RUNS):

            @pl.when(k == 0)
            def _():
                compact(48 * n, 48)

            for m in range(count):
                z_copy(i + m).wait_recv()
            for dx in X_ORDER:
                x_copy(i, count, dx).start()
            if n == 0:
                for m in range(1, NZ):
                    low_z_copy(m, next(i0 for i0, c in RUNS if i0 <= m < i0 + c)).start()

        @pl.when(k >= 1)
        def _():
            for o in range(1, 8):
                remote(lean_rows.at[k - 1, 0], lean_rows.at[k - 1, o], ws.at[k - 1], wr.at[k - 1], owners[o]).start()

        @pl.when(k == 1)
        def _():
            ar_own[0, 1] = reduce_take(0, 0)
            reduce_send(0, 1)

        @pl.when(k == 0)
        def _():
            for i in range(NZ):

                def put(r, value):
                    lent[i, pl.ds(r, SIDE), :] = value

                densify(NZ + i, put)
                lend(i).start()
            for i in range(NZ):

                def keep(r, value):
                    dense[i, pl.ds(r, SIDE), :] = value

                densify(i, keep)

        @pl.when(k == ITERS)
        def _():
            ar_own[1, 0] = local_grams()

        for i, count in ((0, 1),) + RUNS:
            rest = count * (3 * UPPER + (NX * LOWER if i else 0)) // 32
            settle(arrivals.at[pl.ds(0, rest)], xr.at[p, i])

            @pl.when(k == 0)
            def _():
                for n in range(i, i + count):
                    lend(n).wait_recv()

            multiply(acc_far, GROUP * SIDE, i, count)
            if i != RUNS[-1][0]:
                multiply(acc, 0, i, count)

        for dy in (2, 1, 3, 0):
            r = (y + dy) % NY
            halves[p, 0, r] = acc_far[pl.ds(pl.multiple_of(r * SIDE, SIDE), SIDE), :].astype(BF16)
            core_copy(dy).start()
        multiply(acc, 0, *RUNS[-1])

        @pl.when(k == ITERS)
        def _():
            ar_own[1, 0] = ar_own[1, 0] + far_grams()
            reduce_send(1, 0)

        for dy in (2, 1, 3):
            core_copy(dy).wait_recv()
            r = (y + dy) % NY
            both = acc[pl.ds(pl.multiple_of(r * SIDE, SIDE), SIDE), :] + halves[p, 1, r].astype(F32)
            part[p, r] = both.astype(BF16)
            part_copy(dy).start()
        core_copy(0).wait_recv()
        settle(arrivals.at[pl.ds(0, 31 * NX)], gs.at[p])

        @pl.when(k == 1)
        def _():
            sums = spread(reduce_take(0, 1))
            theta[...] = jnp.broadcast_to(DAMPING - sums[0:1] / sums[1:2], (8, SIDE))

        own = acc[pl.ds(pl.multiple_of(y * SIDE, SIDE), SIDE), :] + halves[p, 1, y].astype(F32)
        settle(got.at[p, pl.ds(1, 3)], pr.at[p])
        for o in range(1, NY):
            own = own + got[p, o].astype(F32)
        full = 2.0 * own
        unit = point[...]
        lean = row_sum(unit * full)
        flat = full - lean * unit
        lam[...] = jnp.where(k == 0, jnp.broadcast_to(lean, (SIDE, SIDE)), lam[...])
        before = vs[jnp.maximum(k - 1, 0)]
        new = jnp.where(k == 0, -flat, flat + (DAMPING - theta[0:1, :] - lam[...]) * before)
        vs[k] = new
        gat[1 - p, 0, 0] = new.astype(BF16)

        @pl.when(k == 0)
        def _():
            settle(lent, lent_s)

        return carry

    def lane_sums(terms):
        rows = [jnp.sum(term, axis=0, keepdims=True) for term in terms]
        rows.append(jnp.zeros((16 - len(rows), SIDE), F32))
        sums = jnp.broadcast_to(row_sum(jnp.concatenate(rows, axis=0)), (16, SIDE))
        return jnp.sum(jnp.where(diagonal, sums, 0.0), axis=0, keepdims=True)

    def local_grams():
        pull = (DAMPING - theta[0:1, :] - lam[...]) * vs[2]
        return lane_sums([vs[i] * (vs[j] if j < ITERS else pull) for i, j in PAIRS])

    def far_grams():
        sums = [jnp.zeros((SIDE, SIDE), F32)] * ITERS
        for i in range(ITERS):
            settle(lean_rows.at[i, pl.ds(1, 7)], wr.at[i])
        for b in range(2 * GROUP):
            block = 2.0 * (acc, acc_far)[b // GROUP][b % GROUP * SIDE : (b % GROUP + 1) * SIDE, :]
            o = b // GROUP * NY + (y + NY - b % GROUP) % NY
            for i in range(ITERS):
                sums[i] = sums[i] + lean_rows[i, o].astype(F32) * block
        zero = jnp.zeros((SIDE, SIDE), F32)
        return lane_sums([zero if j < ITERS else sums[i] for i, j in PAIRS])

    lax.fori_loop(0, ITERS + 1, product, 0)

    ar_own[1, 1] = reduce_take(1, 0)
    reduce_send(1, 1)
    total = spread(reduce_take(1, 1))
    gram = {pair: total[e : e + 1, :] for e, pair in enumerate(PAIRS)}
    shift = theta[0:1, :]

    def dot(a, b):
        terms = [a[i] * b[j] * gram[(min(i, j), max(i, j))] for i in a for j in b]
        return functools.reduce(lambda s, t: s + t, terms)

    def axpy(a, scale, b):
        out = dict(a)
        for i, v in b.items():
            out[i] = out[i] + scale * v if i in out else scale * v
        return out

    one = jnp.ones((1, SIDE), F32)
    residual = {0: one}
    direction = {0: one}
    step = {}
    norm_now = dot(residual, residual)
    for turn in range(ITERS):
        image = {i + 1: v for i, v in direction.items()}
        image = axpy(image, shift, direction)
        alpha = norm_now / dot(direction, image)
        step = axpy(step, alpha, direction)
        residual = axpy(residual, -alpha, image)
        if turn < ITERS - 1:
            norm_next = dot(residual, residual)
            direction = axpy(residual, norm_next / norm_now, direction)
            norm_now = norm_next
    out_step[...] = functools.reduce(lambda s, t: s + t, [step[i] * vs[i] for i in sorted(step)])
    out_res[...] = functools.reduce(lambda s, t: s + t, [residual[i] * vs[i] for i in sorted(residual)])

    settle(part.at[1, pl.ds(0, 3)], ps.at[1])
    settle(halves.at[1, 0], hs.at[1])
    for i in range(ITERS):
        settle(lean_rows.at[i, pl.ds(1, 7)], ws.at[i])
    for use in range(2):
        for stage in range(2):
            settle(ar_buf.at[use, stage, pl.ds(1, len(peers[stage]) - 1)], ars.at[use, stage])


def finish(step_ref, res_ref, out_step, out_res):
    out_step[...] = step_ref[...]
    out_res[...] = res_ref[...]


def shards(y_prev, step_prev, accept, blocks, blk_row, blk_col):
    tiles = blocks[0, 0]
    slots = tiles.shape[0]
    vmem = pl.BlockSpec(memory_space=pltpu.VMEM)
    both = pl.pallas_call(
        functools.partial(kernel, slots),
        out_shape=[jax.ShapeDtypeStruct(y_prev.shape, F32)] * 2,
        in_specs=[pl.BlockSpec(memory_space=pl.ANY)] * 6,
        out_specs=[vmem, vmem],
        scratch_shapes=[
            pltpu.VMEM(y_prev.shape, F32),
            pltpu.VMEM(y_prev.shape, F32),
            pltpu.VMEM((1, 1), I32),
            pltpu.VMEM((1, slots), I32),
            pltpu.VMEM((1, slots), I32),
            pltpu.VMEM((slots, SIDE, SIDE), BF16),
            pltpu.VMEM((slots + 1, SIDE, SIDE), BF16),
            pltpu.VMEM((NZ, 2 * GROUP * SIDE, NX * SIDE), BF16),
            pltpu.VMEM((NZ, GROUP * SIDE, NX * SIDE), BF16),
            pltpu.VMEM((TILES * NX, SIDE // NX, SIDE), BF16),
            pltpu.VMEM((2, NZ, NX, SIDE, SIDE), BF16),
            pltpu.VMEM((GROUP * SIDE, SIDE), F32),
            pltpu.VMEM((GROUP * SIDE, SIDE), F32),
            pltpu.VMEM((SIDE, SIDE), F32),
            pltpu.VMEM((SIDE, SIDE), F32),
            pltpu.VMEM((ITERS + 1, SIDE, SIDE), F32),
            pltpu.VMEM((ITERS, 2 * NY, SIDE, SIDE), BF16),
            pltpu.VMEM((2, GROUP, SIDE, SIDE), BF16),
            pltpu.VMEM((2, NY, SIDE, SIDE), BF16),
            pltpu.VMEM((2, 2, GROUP, SIDE, SIDE), BF16),
            pltpu.VMEM((2, 2, 1, SIDE), F32),
            pltpu.VMEM((2, 2, NZ * NX, 1, SIDE), F32),
            pltpu.VMEM((8, SIDE), F32),
            pltpu.VMEM((8, 256), I32),
            pltpu.SMEM((8, 256), I32),
            pltpu.SemaphoreType.DMA((7,)),
            pltpu.SemaphoreType.DMA((2,)),
            pltpu.SemaphoreType.DMA((2, NZ)),
            pltpu.SemaphoreType.DMA((2, NX)),
            pltpu.SemaphoreType.DMA((2, NZ)),
            pltpu.SemaphoreType.DMA,
            pltpu.SemaphoreType.DMA((NZ,)),
            pltpu.SemaphoreType.DMA((ITERS,)),
            pltpu.SemaphoreType.DMA((ITERS,)),
            pltpu.SemaphoreType.DMA((2,)),
            pltpu.SemaphoreType.DMA((2,)),
            pltpu.SemaphoreType.DMA((2,)),
            pltpu.SemaphoreType.DMA((2, NY)),
            pltpu.SemaphoreType.DMA((2, 2)),
            pltpu.SemaphoreType.DMA((2, 2)),
        ],
        compiler_params=pltpu.CompilerParams(
            collective_id=0, has_side_effects=True, vmem_limit_bytes=56 * 1024 * 1024
        ),
        cost_estimate=pl.CostEstimate(flops=4_300_000_000, bytes_accessed=7_000_000, transcendentals=128),
        name="trust_step",
    )(y_prev, step_prev, accept[None], blk_row[0], blk_col[0], tiles)
    return pl.pallas_call(
        finish,
        out_shape=[jax.ShapeDtypeStruct(y_prev.shape, F32)] * 2,
        in_specs=[vmem, vmem],
        out_specs=[vmem, vmem],
        name="finish",
    )(*both)


def solution(mesh):
    placed = (
        P(("row", "col"), None),
        P(("row", "col"), None),
        P(("row", "col")),
        P("row", "col", None, None, None),
        P("row", "col", None),
        P("row", "col", None),
    )
    return jax.shard_map(
        shards,
        mesh=mesh,
        in_specs=placed,
        out_specs=(P(("row", "col"), None), P(("row", "col"), None)),
        check_vma=False,
    )
```

```python
import functools

import jax
import jax.numpy as jnp
from jax import lax
from jax.experimental import pallas as pl
from jax.experimental.pallas import tpu as pltpu
from jax.sharding import PartitionSpec as P

MESH = pl.DeviceIdType.MESH
ITERS = 3
DAMPING = 14.0
NZ, NX, NY = 8, 4, 4
SIDE = 128
GROUP = 4
TILES = 32
UPPER = 96
LOWER = SIDE - UPPER
PLANES = (0, 1, 7, 2, 6, 3, 5, 4)
RUNS = ((1, 2), (3, 2), (5, 2), (7, 1))
X_ORDER = (2, 1, 3)
PAIRS = ((0, 0), (0, 1), (0, 2), (1, 1), (1, 2), (2, 2), (0, 3), (1, 3), (2, 3))
F32 = jnp.float32
BF16 = jnp.bfloat16
I32 = jnp.int32


def device(z, x, core, y):
    return ((z % NZ * NX + x % NX) * 2 + core % 2, y % NY)


def row_sum(a):
    return jnp.sum(a, axis=1, keepdims=True)


def slot_plan(rows, cols, z, x, core):
    slots = rows.shape[1]
    far = jnp.concatenate([rows, jnp.zeros((1, 256 - slots), I32)], axis=1)
    col = jnp.concatenate([cols, jnp.zeros((1, 256 - slots), I32)], axis=1)
    lane = lax.broadcasted_iota(I32, (1, 256), 1)
    dz = (z + NZ - col // 8) % NZ
    dz = jnp.where(dz == 0, 0, jnp.where(dz <= NZ // 2, 2 * dz - 1, 2 * (NZ - dz)))
    dx = (x + NX - (col // 2) % NX) % NX
    rel = (col + core) % 2
    key_row = jnp.where(lane < slots, ((rel * NZ + dz) * NX + dx) * GROUP + far, 1 << 12)
    sub2 = lax.broadcasted_iota(I32, (256, 256), 0)
    lane2 = lax.broadcasted_iota(I32, (256, 256), 1)
    key_r = jnp.broadcast_to(key_row, (256, 256))
    key_col = jnp.sum(jnp.where(sub2 == lane2, key_r, 0), axis=1, keepdims=True)
    key_c = jnp.broadcast_to(key_col, (256, 256))
    same_before = jnp.sum(jnp.where((key_r == key_c) & (lane2 < sub2), 1, 0), axis=1, keepdims=True)
    place = same_before + jnp.sum(jnp.where(key_r < key_c, 1, 0), axis=1, keepdims=True)
    here = jnp.broadcast_to(place, (256, 256)) == lane2
    order = jnp.sum(jnp.where(here, sub2, 0), axis=0, keepdims=True)
    keep = jnp.sum(jnp.where(here & (jnp.broadcast_to(same_before, (256, 256)) > 0), 1, 0), axis=0, keepdims=True)
    upto = jnp.sum(jnp.where(key_c <= lane2, 1, 0), axis=0, keepdims=True)
    found = jnp.sum(jnp.where(key_c == lane2, 1, 0), axis=0, keepdims=True)
    last = jnp.where(found > 0, upto - 1, slots)
    return jnp.concatenate([order, keep, last, jnp.zeros((5, 256), I32)], axis=0)


def kernel(
    slots, y_hbm, step_hbm, accept_hbm, row_hbm, col_hbm, blocks_ref, out_step, out_res,
    y_ref, step_ref, accept_ref, row_ref, col_ref, raw, comp, dense, lent, arrivals, gat, acc, acc_far, point, lam, vs, lean_rows, part, got, halves, ar_own, ar_buf, theta, plan_v, plan_s,
    local_sem, gs, zr, br, xr, lent_s, lent_r, ws, wr, ps, pr, hs, hr, ars, arr,
):
    row = lax.axis_index("row")
    y = lax.axis_index("col")
    z, x, core = row // (2 * NX), row // 2 % NX, row % 2

    plane = [device(z + dz, x + dx, core, y) for dz in range(NZ) for dx in range(NX)]
    owners = [device(z, x, core + j, y + dy) for j in range(2) for dy in range(NY)]
    peers = (plane, owners)
    far_first = [
        sorted(range(1, m * n), key=lambda j: -(min(j // n, m - j // n) + min(j % n, n - j % n)))
        for m, n in ((NZ, NX), (2, NY))
    ]
    greeted = plane[1:NX] + plane[NX::NX] + owners[1:]

    barrier = pltpu.get_barrier_semaphore()
    for peer in greeted:
        pl.semaphore_signal(barrier, inc=1, device_id=peer, device_id_type=MESH)
    pairs = ((y_hbm, y_ref), (step_hbm, step_ref), (accept_hbm, accept_ref), (row_hbm, row_ref), (col_hbm, col_ref))
    small = [pltpu.make_async_copy(src, dst, local_sem.at[2 + n]) for n, (src, dst) in enumerate(pairs)]
    for copy in small:
        copy.start()
    blocks_copy = pltpu.make_async_copy(blocks_ref, raw, local_sem.at[0])
    blocks_copy.start()
    for copy in small:
        copy.wait()

    moved = y_ref[...] + accept_ref[...].astype(F32) * step_ref[...]
    unit = moved * lax.rsqrt(row_sum(moved * moved) + 1e-06)
    point[...] = unit
    gat[0, 0, 0] = unit.astype(BF16)
    vs[0] = jnp.zeros((SIDE, SIDE), F32)
    lam[...] = jnp.zeros((SIDE, SIDE), F32)
    theta[...] = jnp.zeros((8, SIDE), F32)
    out_res[...] = jnp.zeros((SIDE, SIDE), F32)
    plan_copy = pltpu.make_async_copy(plan_v, plan_s, local_sem.at[1])
    comp[slots] = jnp.zeros((SIDE, SIDE), BF16)
    pl.semaphore_wait(barrier, len(greeted))

    diagonal = lax.broadcasted_iota(I32, (16, SIDE), 0) == lax.broadcasted_iota(I32, (16, SIDE), 1)

    def remote(src, dst, send, recv, peer):
        return pltpu.make_async_remote_copy(
            src_ref=src, dst_ref=dst, send_sem=send, recv_sem=recv, device_id=peer, device_id_type=MESH
        )

    def settle(ref, sem):
        pltpu.make_async_copy(ref, ref, sem).wait()

    def reduce_send(use, stage):
        for j in far_first[stage]:
            remote(
                ar_own.at[use, stage], ar_buf.at[use, stage, j], ars.at[use, stage], arr.at[use, stage], peers[stage][j]
            ).start()

    def reduce_take(use, stage):
        count = len(peers[stage])
        settle(ar_buf.at[use, stage, pl.ds(1, count - 1)], arr.at[use, stage])
        return ar_own[use, stage] + jnp.sum(ar_buf[use, stage, 1:count], axis=0)

    def spread(total):
        return jnp.broadcast_to(row_sum(jnp.where(diagonal, jnp.broadcast_to(total, (16, SIDE)), 0.0)), (16, SIDE))

    def compact(start, count):
        def one(j, total):
            total = plan_s[1, j].astype(F32) * total + raw[plan_s[0, j]].astype(F32)
            comp[j] = total.astype(BF16)
            return total

        out_res[...] = lax.fori_loop(start, start + count, one, out_res[...])

    def densify(chunk, store):
        def one(r, carry):
            store(
                pl.multiple_of(r * SIDE, SIDE),
                jnp.concatenate([comp[plan_s[2, chunk * 16 + i * GROUP + r]] for i in range(NX)], axis=1),
            )
            return carry

        lax.fori_loop(0, GROUP, one, 0)

    def lend(d):
        return remote(lent.at[d], dense.at[d, pl.ds(GROUP * SIDE, GROUP * SIDE)], lent_s, lent_r.at[d], owners[NY])

    def product(k, carry):
        p = k % 2

        def high(i, count, dx):
            return gat.at[p, pl.ds(i, count), dx, pl.ds(0, UPPER)]

        def low(i, dx, count):
            return gat.at[p, i, pl.ds(dx, count), pl.ds(UPPER, LOWER)]

        def z_copy(i):
            return remote(high(0, 1, 0), high(i, 1, 0), gs.at[p], zr.at[p, i], device(z + PLANES[i], x, core, y))

        def x_copy(i, count, dx):
            return remote(high(i, count, 0), high(i, count, dx), gs.at[p], xr.at[p, i], device(z, x + dx, core, y))

        def low_x_copy(dx):
            return remote(low(0, 0, 1), low(0, dx, 1), gs.at[p], br.at[p, dx], device(z, x + dx, core, y))

        def low_z_copy(i, run):
            return remote(low(0, 0, NX), low(i, 0, NX), gs.at[p], xr.at[p, run], device(z + PLANES[i], x, core, y))

        def part_copy(o):
            return remote(part.at[p, (y + o) % NY], got.at[p, o], ps.at[p], pr.at[p], owners[o])

        def core_copy(dy):
            r = (y + dy) % NY
            return remote(halves.at[p, 0, r], halves.at[p, 1, r], hs.at[p], hr.at[p, dy], owners[NY])

        def multiply(total, at, i, count):
            term = functools.reduce(
                lambda s, t: s + t,
                [
                    jnp.dot(
                        dense[n, at : at + GROUP * SIDE],
                        gat[p, n].reshape(NX * SIDE, SIDE),
                        preferred_element_type=F32,
                    )
                    for n in range(i, i + count)
                ],
            )
            total[...] = total[...] + term if i else term

        for i in range(1, NZ):
            z_copy(i).start()
        for dx in (1, 3, 2):
            low_x_copy(dx).start()
        for dx in X_ORDER:
            x_copy(0, 1, dx).start()

        @pl.when(k >= 1)
        def _():
            settle(part.at[1 - p, pl.ds(0, 3)], ps.at[1 - p])
            settle(halves.at[1 - p, 0], hs.at[1 - p])
            new = vs[k - 1]
            lean_rows[k - 1, 0] = (new - row_sum(point[...] * new) * point[...]).astype(BF16)


        @pl.when(k == 0)
        def _():
            plan_v[...] = slot_plan(row_ref[...], col_ref[...], z, x, core)
            plan_copy.start()

        for dx in (1, 3, 2):
            low_x_copy(dx).wait_recv()

        @pl.when(k == 0)
        def _():
            plan_copy.wait()
            blocks_copy.wait()

        for n, (i, count) in enumerate(RUNS):

            @pl.when(k == 0)
            def _():
                compact(48 * n, 48)

            for m in range(count):
                z_copy(i + m).wait_recv()
            for dx in X_ORDER:
                x_copy(i, count, dx).start()
            if n == 0:
                for m in range(1, NZ):
                    low_z_copy(m, next(i0 for i0, c in RUNS if i0 <= m < i0 + c)).start()

        @pl.when(k >= 1)
        def _():
            for o in range(1, 8):
                remote(lean_rows.at[k - 1, 0], lean_rows.at[k - 1, o], ws.at[k - 1], wr.at[k - 1], owners[o]).start()

        @pl.when(k == 1)
        def _():
            square = vs[0] * vs[0]
            ar_own[0, 0] = lane_sums([lam[...] * square, square])
            reduce_send(0, 0)

        @pl.when(k == 0)
        def _():
            for i in range(NZ):

                def put(r, value):
                    lent[i, pl.ds(r, SIDE), :] = value

                densify(NZ + i, put)
                lend(i).start()
            for i in range(NZ):

                def keep(r, value):
                    dense[i, pl.ds(r, SIDE), :] = value

                densify(i, keep)

        @pl.when(k == ITERS)
        def _():
            ar_own[1, 0] = local_grams()

        for i, count in ((0, 1),) + RUNS:
            rest = count * (3 * UPPER + (NX * LOWER if i else 0)) // 32
            settle(arrivals.at[pl.ds(0, rest)], xr.at[p, i])

            @pl.when(k == 0)
            def _():
                for n in range(i, i + count):
                    lend(n).wait_recv()

            multiply(acc_far, GROUP * SIDE, i, count)
            if i != RUNS[-1][0]:
                multiply(acc, 0, i, count)

        for dy in (2, 1, 3, 0):
            r = (y + dy) % NY
            halves[p, 0, r] = acc_far[pl.ds(pl.multiple_of(r * SIDE, SIDE), SIDE), :].astype(BF16)
            core_copy(dy).start()
        @pl.when(k == 1)
        def _():
            ar_own[0, 1] = reduce_take(0, 0)
            reduce_send(0, 1)

        multiply(acc, 0, *RUNS[-1])

        @pl.when(k == ITERS)
        def _():
            ar_own[1, 0] = ar_own[1, 0] + far_grams()
            reduce_send(1, 0)

        for dy in (2, 1, 3):
            core_copy(dy).wait_recv()
            r = (y + dy) % NY
            both = acc[pl.ds(pl.multiple_of(r * SIDE, SIDE), SIDE), :] + halves[p, 1, r].astype(F32)
            part[p, r] = both.astype(BF16)
            part_copy(dy).start()
        core_copy(0).wait_recv()
        settle(arrivals.at[pl.ds(0, 31 * NX)], gs.at[p])

        @pl.when(k == 1)
        def _():
            sums = spread(reduce_take(0, 1))
            theta[...] = jnp.broadcast_to(DAMPING - sums[0:1] / sums[1:2], (8, SIDE))

        own = acc[pl.ds(pl.multiple_of(y * SIDE, SIDE), SIDE), :] + halves[p, 1, y].astype(F32)
        settle(got.at[p, pl.ds(1, 3)], pr.at[p])
        for o in range(1, NY):
            own = own + got[p, o].astype(F32)
        full = 2.0 * own
        unit = point[...]
        lean = row_sum(unit * full)
        flat = full - lean * unit
        lam[...] = jnp.where(k == 0, jnp.broadcast_to(lean, (SIDE, SIDE)), lam[...])
        before = vs[jnp.maximum(k - 1, 0)]
        new = jnp.where(k == 0, -flat, flat + (DAMPING - theta[0:1, :] - lam[...]) * before)
        vs[k] = new
        gat[1 - p, 0, 0] = new.astype(BF16)

        @pl.when(k == 0)
        def _():
            settle(lent, lent_s)

        return carry

    def lane_sums(terms):
        rows = [jnp.sum(term, axis=0, keepdims=True) for term in terms]
        rows.append(jnp.zeros((16 - len(rows), SIDE), F32))
        sums = jnp.broadcast_to(row_sum(jnp.concatenate(rows, axis=0)), (16, SIDE))
        return jnp.sum(jnp.where(diagonal, sums, 0.0), axis=0, keepdims=True)

    def local_grams():
        pull = (DAMPING - theta[0:1, :] - lam[...]) * vs[2]
        return lane_sums([vs[i] * (vs[j] if j < ITERS else pull) for i, j in PAIRS])

    def far_grams():
        sums = [jnp.zeros((SIDE, SIDE), F32)] * ITERS
        for i in range(ITERS):
            settle(lean_rows.at[i, pl.ds(1, 7)], wr.at[i])
        for b in range(2 * GROUP):
            block = 2.0 * (acc, acc_far)[b // GROUP][b % GROUP * SIDE : (b % GROUP + 1) * SIDE, :]
            o = b // GROUP * NY + (y + NY - b % GROUP) % NY
            for i in range(ITERS):
                sums[i] = sums[i] + lean_rows[i, o].astype(F32) * block
        zero = jnp.zeros((SIDE, SIDE), F32)
        return lane_sums([zero if j < ITERS else sums[i] for i, j in PAIRS])

    lax.fori_loop(0, ITERS + 1, product, 0)

    ar_own[1, 1] = reduce_take(1, 0)
    reduce_send(1, 1)
    total = spread(reduce_take(1, 1))
    gram = {pair: total[e : e + 1, :] for e, pair in enumerate(PAIRS)}
    shift = theta[0:1, :]

    def dot(a, b):
        terms = [a[i] * b[j] * gram[(min(i, j), max(i, j))] for i in a for j in b]
        return functools.reduce(lambda s, t: s + t, terms)

    def axpy(a, scale, b):
        out = dict(a)
        for i, v in b.items():
            out[i] = out[i] + scale * v if i in out else scale * v
        return out

    one = jnp.ones((1, SIDE), F32)
    residual = {0: one}
    direction = {0: one}
    step = {}
    norm_now = dot(residual, residual)
    for turn in range(ITERS):
        image = {i + 1: v for i, v in direction.items()}
        image = axpy(image, shift, direction)
        alpha = norm_now / dot(direction, image)
        step = axpy(step, alpha, direction)
        residual = axpy(residual, -alpha, image)
        if turn < ITERS - 1:
            norm_next = dot(residual, residual)
            direction = axpy(residual, norm_next / norm_now, direction)
            norm_now = norm_next
    out_step[...] = functools.reduce(lambda s, t: s + t, [step[i] * vs[i] for i in sorted(step)])
    out_res[...] = functools.reduce(lambda s, t: s + t, [residual[i] * vs[i] for i in sorted(residual)])

    settle(part.at[1, pl.ds(0, 3)], ps.at[1])
    settle(halves.at[1, 0], hs.at[1])
    for i in range(ITERS):
        settle(lean_rows.at[i, pl.ds(1, 7)], ws.at[i])
    for use in range(2):
        for stage in range(2):
            settle(ar_buf.at[use, stage, pl.ds(1, len(peers[stage]) - 1)], ars.at[use, stage])


def finish(step_ref, res_ref, out_step, out_res):
    out_step[...] = step_ref[...]
    out_res[...] = res_ref[...]


def shards(y_prev, step_prev, accept, blocks, blk_row, blk_col):
    tiles = blocks[0, 0]
    slots = tiles.shape[0]
    vmem = pl.BlockSpec(memory_space=pltpu.VMEM)
    both = pl.pallas_call(
        functools.partial(kernel, slots),
        out_shape=[jax.ShapeDtypeStruct(y_prev.shape, F32)] * 2,
        in_specs=[pl.BlockSpec(memory_space=pl.ANY)] * 6,
        out_specs=[vmem, vmem],
        scratch_shapes=[
            pltpu.VMEM(y_prev.shape, F32),
            pltpu.VMEM(y_prev.shape, F32),
            pltpu.VMEM((1, 1), I32),
            pltpu.VMEM((1, slots), I32),
            pltpu.VMEM((1, slots), I32),
            pltpu.VMEM((slots, SIDE, SIDE), BF16),
            pltpu.VMEM((slots + 1, SIDE, SIDE), BF16),
            pltpu.VMEM((NZ, 2 * GROUP * SIDE, NX * SIDE), BF16),
            pltpu.VMEM((NZ, GROUP * SIDE, NX * SIDE), BF16),
            pltpu.VMEM((TILES * NX, SIDE // NX, SIDE), BF16),
            pltpu.VMEM((2, NZ, NX, SIDE, SIDE), BF16),
            pltpu.VMEM((GROUP * SIDE, SIDE), F32),
            pltpu.VMEM((GROUP * SIDE, SIDE), F32),
            pltpu.VMEM((SIDE, SIDE), F32),
            pltpu.VMEM((SIDE, SIDE), F32),
            pltpu.VMEM((ITERS + 1, SIDE, SIDE), F32),
            pltpu.VMEM((ITERS, 2 * NY, SIDE, SIDE), BF16),
            pltpu.VMEM((2, GROUP, SIDE, SIDE), BF16),
            pltpu.VMEM((2, NY, SIDE, SIDE), BF16),
            pltpu.VMEM((2, 2, GROUP, SIDE, SIDE), BF16),
            pltpu.VMEM((2, 2, 1, SIDE), F32),
            pltpu.VMEM((2, 2, NZ * NX, 1, SIDE), F32),
            pltpu.VMEM((8, SIDE), F32),
            pltpu.VMEM((8, 256), I32),
            pltpu.SMEM((8, 256), I32),
            pltpu.SemaphoreType.DMA((7,)),
            pltpu.SemaphoreType.DMA((2,)),
            pltpu.SemaphoreType.DMA((2, NZ)),
            pltpu.SemaphoreType.DMA((2, NX)),
            pltpu.SemaphoreType.DMA((2, NZ)),
            pltpu.SemaphoreType.DMA,
            pltpu.SemaphoreType.DMA((NZ,)),
            pltpu.SemaphoreType.DMA((ITERS,)),
            pltpu.SemaphoreType.DMA((ITERS,)),
            pltpu.SemaphoreType.DMA((2,)),
            pltpu.SemaphoreType.DMA((2,)),
            pltpu.SemaphoreType.DMA((2,)),
            pltpu.SemaphoreType.DMA((2, NY)),
            pltpu.SemaphoreType.DMA((2, 2)),
            pltpu.SemaphoreType.DMA((2, 2)),
        ],
        compiler_params=pltpu.CompilerParams(
            collective_id=0, has_side_effects=True, vmem_limit_bytes=56 * 1024 * 1024
        ),
        cost_estimate=pl.CostEstimate(flops=4_300_000_000, bytes_accessed=7_000_000, transcendentals=128),
        name="trust_step",
    )(y_prev, step_prev, accept[None], blk_row[0], blk_col[0], tiles)
    return pl.pallas_call(
        finish,
        out_shape=[jax.ShapeDtypeStruct(y_prev.shape, F32)] * 2,
        in_specs=[vmem, vmem],
        out_specs=[vmem, vmem],
        name="finish",
    )(*both)


def solution(mesh):
    placed = (
        P(("row", "col"), None),
        P(("row", "col"), None),
        P(("row", "col")),
        P("row", "col", None, None, None),
        P("row", "col", None),
        P("row", "col", None),
    )
    return jax.shard_map(
        shards,
        mesh=mesh,
        in_specs=placed,
        out_specs=(P(("row", "col"), None), P(("row", "col"), None)),
        check_vma=False,
    )
```
